256 devices in a mesh: gx: 4 (over z_hi), gy: 8 (over z_lo, x), gz: 8 (over y, core).
Axes of the slice: x: 4, y: 4, z: 8 (z_hi: 4, z_lo: 2; z = z_hi * 2 + z_lo), core: 2. Of those that a mesh axis runs over, the one named last changes fastest.
Arguments:
- spectrum_real: float32 [512, 512, 512], P(None, ('gx', 'gy', 'gz')), may hold values from -6 to 6
- spectrum_imag: float32 [512, 512, 512], P(None, ('gx', 'gy', 'gz')), may hold values from -6 to 6
- volume: float32 [512, 512, 512], P('gy', 'gz', 'gx'), may hold values from -6 to 6
- weights: float32 [512, 512, 512], P('gy', 'gz', 'gx'), may hold values from 0.3 to 3
Outputs:
- updated: float32 [512, 512, 512], P('gy', 'gz', 'gx')
The draws below stay inside these ranges and needn't reach their ends.
All inputs are finite; a program needn't handle non-finite values.
Results may differ from the reference program's by a relative error of at most 0.000075.
Values sent between devices are 32-bit elements; how exact they have to be, the bound alone decides.
A program may use at most 128 MiB of HBM per device.

```python
import math
import jax
import jax.numpy as jnp
from jax import lax

NY = 512
NZ = 512
NX = 512


def block_scale(key, dims, split, low, top_value):
    factor_of, own = 1.0, jax.random.fold_in(key, 6)
    for dim, blocks in split:
        steps = jnp.exp(jax.random.uniform(jax.random.fold_in(own, dim), (blocks,), jnp.float32, low / len(split), top_value / len(split)))
        factor_of = factor_of * jnp.repeat(steps, dims[dim] // blocks).reshape([-1 if axis == dim else 1 for axis in range(len(dims))])
    return factor_of


def bell_draw(own_key, dims, width, bound, cuts=(), kind=jnp.bfloat16):
    drawn = jax.random.normal(own_key, dims, jnp.float32) * width
    if len(cuts) > 0:
        drawn = block_scale(own_key, dims, cuts, -0.22, 0.18) * drawn
    return jnp.clip(drawn, min=-bound, max=bound).astype(kind)


def setup_inputs(seed: int = 0) -> dict:
    seeds = jax.random.split(jax.random.key(seed), 5)
    spectrum_real = bell_draw(seeds[0], (NY, NZ, NX), 1.0, 6.0, ((1, 256),), jnp.float32)
    spectrum_imag = bell_draw(seeds[1], (NY, NZ, NX), 1.0, 6.0, ((1, 256),), jnp.float32)
    volume = bell_draw(seeds[2], (NY, NZ, NX), 1.0, 6.0, ((0, 8), (1, 8), (2, 4)), jnp.float32)
    weights = jnp.clip(jnp.exp(math.log(3.0) - 2.3025851 * jax.random.uniform(seeds[3], (NY, NZ, NX), jnp.float32) ** block_scale(seeds[3], (NY, NZ, NX), ((0, 8), (1, 8), (2, 4)), -0.2, 0.2)), 0.3, 3.0)
    return {"spectrum_real": spectrum_real, "spectrum_imag": spectrum_imag, "volume": volume, "weights": weights}


step_size = 0.5
tv_weight = 0.5
smoothing = 0.5

def forward_slope(field, which):
    length = field.shape[which]
    ahead = jnp.concatenate([lax.slice_in_dim(field, 1, length, axis=which), lax.slice_in_dim(field, length - 1, length, axis=which)], axis=which)
    return ahead - field

def previous_voxel(field, which):
    length = field.shape[which]
    zeros = jnp.zeros_like(lax.slice_in_dim(field, 0, 1, axis=which))
    return jnp.concatenate([zeros, lax.slice_in_dim(field, 0, length - 1, axis=which)], axis=which)

def reference(spectrum_real, spectrum_imag, volume, weights):
    spectrum = lax.complex(spectrum_real, spectrum_imag)
    data_term = jnp.real(jnp.fft.ifftn(spectrum, norm='ortho')).astype(volume.dtype)
    slopes = [forward_slope(volume, which) for which in range(3)]
    magnitude = jnp.sqrt(slopes[0] * slopes[0] + slopes[1] * slopes[1] + slopes[2] * slopes[2] + smoothing)
    scaled = weights / magnitude
    tv_grad = jnp.zeros_like(volume)
    for which in range(3):
        flux = scaled * slopes[which]
        tv_grad = tv_grad + previous_voxel(flux, which) - flux
    return volume - step_size * (data_term + tv_weight * tv_grad)
```

```python
import functools
import math

import jax
import jax.numpy as jnp
import ml_dtypes
import numpy as np
from jax import lax
from jax.experimental import pallas as pl
from jax.experimental.pallas import tpu as pltpu
from jax.sharding import PartitionSpec as P

step_size = 0.5
tv_weight = 0.5
smoothing = 0.5
MESH = pl.DeviceIdType.MESH
X_CHIPS = 4


def padded_2(x, sides, width):
    for axis, dim in sides:
        size, length = (lax.axis_size(axis), x.shape[dim])
        up = [(i, (i + 1) % size) for i in range(size - 1)]
        down = [(j, i) for i, j in up]
        last = lax.slice_in_dim(x, length - width, length, axis=dim)
        initial = lax.slice_in_dim(x, 0, width, axis=dim)
        before = lax.ppermute(last, axis, up)
        after = lax.ppermute(initial, axis, down)
        x = jnp.concatenate([before, x, after], axis=dim)
    return x


def region(field, start_y, start_z, start_x, size_y, size_z, size_x):
    return field[start_y : start_y + size_y, start_z : start_z + size_z, start_x : start_x + size_x]


def tv_gradient(volume, weights):
    stacked = jnp.stack([volume, weights])
    padded = padded_2(stacked, (("gx", 3), ("gy", 1), ("gz", 2)), 1)
    brick_y, brick_z, brick_x = volume.shape
    end_y, end_z, end_x = (n * lax.axis_size(a) for n, a in zip(volume.shape, ("gy", "gz", "gx")))
    span_y, span_z, span_x = (brick_y + 1, brick_z + 1, brick_x + 1)
    field = padded[0]
    edge_weights = padded[1]
    base = region(field, 0, 0, 0, span_y, span_z, span_x)
    global_y = lax.axis_index("gy") * brick_y + jnp.arange(span_y, dtype=jnp.int32) - 1
    global_z = lax.axis_index("gz") * brick_z + jnp.arange(span_z, dtype=jnp.int32) - 1
    global_x = lax.axis_index("gx") * brick_x + jnp.arange(span_x, dtype=jnp.int32) - 1
    slope_y = region(field, 1, 0, 0, span_y, span_z, span_x) - base
    slope_z = region(field, 0, 1, 0, span_y, span_z, span_x) - base
    slope_x = region(field, 0, 0, 1, span_y, span_z, span_x) - base
    slope_y = jnp.where((global_y < end_y - 1)[:, None, None], slope_y, 0.0)
    slope_z = jnp.where((global_z < end_z - 1)[None, :, None], slope_z, 0.0)
    slope_x = jnp.where((global_x < end_x - 1)[None, None, :], slope_x, 0.0)
    magnitude = jnp.sqrt(slope_y * slope_y + slope_z * slope_z + slope_x * slope_x + smoothing)
    inside = (
        (global_y >= 0)[:, None, None]
        & (global_z >= 0)[None, :, None]
        & (global_x >= 0)[None, None, :]
    )
    scaled = jnp.where(
        inside, region(edge_weights, 0, 0, 0, span_y, span_z, span_x) / magnitude, 0.0
    )
    flux_y = scaled * slope_y
    flux_z = scaled * slope_z
    flux_x = scaled * slope_x
    tv_grad = flux_y[:-1, 1:, 1:] - flux_y[1:, 1:, 1:]
    tv_grad = tv_grad + flux_z[1:, :-1, 1:] - flux_z[1:, 1:, 1:]
    tv_grad = tv_grad + flux_x[1:, 1:, :-1] - flux_x[1:, 1:, 1:]
    return tv_grad


def halves(table):
    high = table.astype(ml_dtypes.bfloat16)
    low = (table - high.astype(np.float64)).astype(ml_dtypes.bfloat16)
    return np.stack([high, low])


def cos_sin(length, rows, columns):
    phases = (np.asarray(rows)[:, None] * np.asarray(columns)[None, :]) % length
    angles = phases * (2.0 * math.pi / length)
    factor = 1.0 / math.sqrt(length)
    return np.cos(angles) * factor, np.sin(angles) * factor


class Sizes:
    def __init__(self, mesh_sizes, x_chips, ny, nz, nx):
        self.gx, self.gy, self.gz = mesh_sizes
        self.ny, self.nz, self.nx = ny, nz, nx
        self.plane = self.gx * self.gy
        self.planes = nz // (self.plane * self.gz)
        self.chips = x_chips
        self.ring = self.plane // x_chips
        self.by, self.bz, self.bx = ny // self.gy, nz // self.gz, nx // self.gx
        self.rows = self.by // self.gz
        self.lines = 2 * nz


def make_tables(s):
    c, n = cos_sin(s.nx, range(s.nx), range(s.nx))
    table_x = halves(np.concatenate([c, n], axis=0))
    c, n = cos_sin(s.ny, range(s.ny), range(s.ny))
    table_y = halves(np.concatenate([c, n], axis=1))
    k, r, g, x = np.meshgrid(
        range(s.planes), range(s.ring), range(s.gz), range(s.chips), indexing="ij"
    )
    kz = (((r * s.chips + x) * s.gz + g) * s.planes + k).reshape(-1)
    c, n = cos_sin(s.nz, range(s.nz), kz)
    table_z = halves(np.stack([c, -n], axis=-1).reshape(s.nz, s.lines))
    return table_x, table_y, table_z


def split(x):
    high = x.astype(jnp.bfloat16)
    return high, (x - high.astype(jnp.float32)).astype(jnp.bfloat16)


def dot3(a_high, a_low, b_high, b_low):
    f32 = jnp.float32
    return (
        jnp.dot(a_high, b_high, preferred_element_type=f32)
        + jnp.dot(a_high, b_low, preferred_element_type=f32)
        + jnp.dot(a_low, b_high, preferred_element_type=f32)
    )


def kernel(
    s, sr, si, tx, ty, tz, out,
    mid, mine, blocks, pencils, lines, bricks,
    send1, recv1, send2, recv2, send3, recv3,
):
    gx, gy, gz = lax.axis_index("gx"), lax.axis_index("gy"), lax.axis_index("gz")
    here = gx * s.gy + gy
    ring, chip = here // s.chips, here % s.chips
    half = s.nx
    lanes = s.nx // 128
    tile_y = min(256, s.ny)
    chunk = min(128, s.ny)

    def place(index):
        return (index // s.gy, index % s.gy, gz)

    def beside(step):
        return (gx, gy, (gz + step) % s.gz)

    barrier = pltpu.get_barrier_semaphore()

    def greet(i, _):
        pl.semaphore_signal(barrier, inc=1, device_id=place((here + i) % s.plane), device_id_type=MESH)
        return 0

    def greet_beside(i, _):
        pl.semaphore_signal(barrier, inc=1, device_id=beside(i), device_id_type=MESH)
        return 0

    lax.fori_loop(1, s.plane, greet, 0)
    lax.fori_loop(1, s.gz, greet_beside, 0)

    def transform_x(k):
        def body(t, _):
            def plane_rows(ref):
                first = t * chunk * lanes * s.planes + k
                return jnp.concatenate(
                    [
                        ref[pl.ds(first + j * s.planes, chunk, stride=lanes * s.planes), :]
                        for j in range(lanes)
                    ],
                    axis=1,
                )

            re_high, re_low = split(plane_rows(sr))
            im_high, im_low = split(plane_rows(si))
            high = jnp.concatenate(
                [jnp.concatenate([re_high, -im_high], 1), jnp.concatenate([im_high, re_high], 1)], 0
            )
            low = jnp.concatenate(
                [jnp.concatenate([re_low, -im_low], 1), jnp.concatenate([im_low, re_low], 1)], 0
            )
            both = dot3(high, low, tx[0], tx[1])
            re_high, re_low = split(both[:chunk])
            im_high, im_low = split(both[chunk:])
            at = pl.multiple_of(t * chunk, chunk)
            mid[0, pl.ds(at, chunk), :] = im_high
            mid[1, pl.ds(at, chunk), :] = im_low
            mid[0, pl.ds(s.ny + at, chunk), :] = re_high
            mid[1, pl.ds(s.ny + at, chunk), :] = re_low
            mid[0, pl.ds(2 * s.ny + at, chunk), :] = -im_high
            mid[1, pl.ds(2 * s.ny + at, chunk), :] = -im_low
            return 0

        lax.fori_loop(0, s.ny // chunk, body, 0)

    def transform_y(k):
        per = tile_y // s.by

        def body(t, _):
            at = pl.multiple_of(t * tile_y, tile_y)
            high, low = ty[0, pl.ds(at, tile_y), :], ty[1, pl.ds(at, tile_y), :]
            for c, first in ((0, s.ny), (1, 0)):
                o = dot3(
                    high, low, mid[0, first : first + 2 * s.ny, :], mid[1, first : first + 2 * s.ny, :]
                )
                for q in range(s.gx):
                    mine[pl.ds(q * s.gy + t * per, per), k, c] = o[
                        :, q * 128 : (q + 1) * 128
                    ].reshape(per, s.by, 128)
            return 0

        lax.fori_loop(0, s.ny // tile_y, body, 0)

    turns = []
    for h in range(1, s.ring // 2 + 1):
        turns += [h] if 2 * h == s.ring else [h, s.ring - h]

    def send_block(k, turn, dx):
        to = ((ring + turn) % s.ring) * s.chips + (chip + dx) % s.chips
        pltpu.make_async_remote_copy(
            src_ref=mine.at[to, k],
            dst_ref=blocks.at[k, pl.ds(2 * here, 2)],
            send_sem=send1,
            recv_sem=recv1.at[k, ring],
            device_id=place(to),
            device_id_type=MESH,
        ).start()

    def plane(k, _):
        transform_x(k)
        transform_y(k)

        @pl.when(k == 0)
        def _():
            pl.semaphore_wait(barrier, s.plane - 1 + s.gz - 1)

        for turn in turns:
            lax.fori_loop(0, s.chips, lambda dx, _: (send_block(k, turn, dx), 0)[1], 0)
        lax.fori_loop(1, s.chips, lambda dx, _: (send_block(k, 0, dx), 0)[1], 0)
        pltpu.make_async_copy(
            mine.at[here, k], blocks.at[k, pl.ds(2 * here, 2)], recv1.at[k, ring]
        ).start()
        return 0

    lax.fori_loop(0, s.planes, plane, 0)

    width = 2 * s.chips

    def forward(k, _):
        for turn in turns + [0]:
            source = (ring + s.ring - turn) % s.ring
            group = blocks.at[k, pl.ds(source * width, width)]
            pltpu.make_async_copy(group, group, recv1.at[k, source]).wait()

            def step(i, _):
                to = (gz + i) % s.gz
                pltpu.make_async_remote_copy(
                    src_ref=group.at[:, pl.ds(to * s.rows, s.rows), :],
                    dst_ref=pencils.at[pl.ds(((k * s.ring + source) * s.gz + gz) * width, width)],
                    send_sem=send2,
                    recv_sem=recv2,
                    device_id=beside(i),
                    device_id_type=MESH,
                ).start()
                return 0

            lax.fori_loop(1, s.gz, step, 0)
            pltpu.make_async_copy(
                group.at[:, pl.ds(gz * s.rows, s.rows), :],
                pencils.at[pl.ds(((k * s.ring + source) * s.gz + gz) * width, width)],
                recv2,
            ).start()
        return 0

    lax.fori_loop(0, s.planes, forward, 0)
    pltpu.make_async_copy(pencils, pencils, recv2).wait()

    tile_z = min(256, s.nz)

    def transform_z(pair, _):
        pieces = [
            split(pencils[:, 2 * pair + j, :]) for j in range(2)
        ]
        high = jnp.concatenate([p[0] for p in pieces], axis=1)
        low = jnp.concatenate([p[1] for p in pieces], axis=1)
        for t in range(s.nz // tile_z):
            at = slice(t * tile_z, (t + 1) * tile_z)
            o = dot3(tz[0, at, :], tz[1, at, :], high, low)
            for j in range(2):
                lines[2 * pair + j, at, :] = o[:, j * 128 : (j + 1) * 128]

        def step(i, _):
            to = (gz + i) % s.gz
            pltpu.make_async_remote_copy(
                src_ref=lines.at[pl.ds(2 * pair, 2), pl.ds(to * s.bz, s.bz), :],
                dst_ref=bricks.at[gz, pl.ds(2 * pair, 2)],
                send_sem=send3,
                recv_sem=recv3,
                device_id=beside(i),
                device_id_type=MESH,
            ).start()
            return 0

        lax.fori_loop(1, s.gz, step, 0)
        pltpu.make_async_copy(
            lines.at[pl.ds(2 * pair, 2), pl.ds(gz * s.bz, s.bz), :],
            bricks.at[gz, pl.ds(2 * pair, 2)],
            recv3,
        ).start()
        return 0

    lax.fori_loop(0, s.rows // 2, transform_z, 0)
    pltpu.make_async_copy(bricks, bricks, recv3).wait()
    out[...] = bricks[...].reshape(out.shape)

    sent = mine.at[pl.ds(0, s.plane - 1)]
    pltpu.make_async_copy(sent, sent, send1).wait()
    sent = pencils.at[pl.ds(0, s.lines // s.gz * (s.gz - 1))]
    pltpu.make_async_copy(sent, sent, send2).wait()
    sent = bricks.at[pl.ds(0, s.gz - 1)]
    pltpu.make_async_copy(sent, sent, send3).wait()


def data_term(s, spectrum_real, spectrum_imag):
    tables = make_tables(s)

    def rows(x):
        x = x.reshape(s.ny, s.planes, s.nx // 128, 128)
        return x.transpose(0, 2, 1, 3).reshape(-1, 128)

    f32 = jnp.float32
    return pl.pallas_call(
        functools.partial(kernel, s),
        out_shape=jax.ShapeDtypeStruct((s.by, s.bz, s.bx), f32),
        in_specs=[pl.BlockSpec(memory_space=pltpu.VMEM)] * 5,
        out_specs=pl.BlockSpec(memory_space=pltpu.VMEM),
        scratch_shapes=[
            pltpu.VMEM((2, 3 * s.ny, s.nx), jnp.bfloat16),
            pltpu.VMEM((s.plane, s.planes, 2, s.by, 128), f32),
            pltpu.VMEM((s.planes, 2 * s.plane, s.by, 128), f32),
            pltpu.VMEM((s.lines, s.rows, 128), f32),
            pltpu.VMEM((s.rows, s.nz, 128), f32),
            pltpu.VMEM((s.gz, s.rows, s.bz, 128), f32),
            pltpu.SemaphoreType.DMA,
            pltpu.SemaphoreType.DMA((s.planes, s.ring)),
            pltpu.SemaphoreType.DMA,
            pltpu.SemaphoreType.DMA,
            pltpu.SemaphoreType.DMA,
            pltpu.SemaphoreType.DMA,
        ],
        compiler_params=pltpu.CompilerParams(
            collective_id=0, has_side_effects=True, vmem_limit_bytes=60 * 1024 * 1024
        ),
    )(rows(spectrum_real), rows(spectrum_imag), *(jnp.asarray(t) for t in tables))


def on_device(s, spectrum_real, spectrum_imag, volume, weights):
    tv_grad = tv_gradient(volume, weights)
    data = data_term(s, spectrum_real, spectrum_imag)
    return volume - step_size * (data + tv_weight * tv_grad)


def build(mesh, x_chips, shape):
    sizes = Sizes([mesh.shape[a] for a in ("gx", "gy", "gz")], x_chips, *shape)
    spectrum, brick = P(None, ("gx", "gy", "gz"), None), P("gy", "gz", "gx")
    return jax.shard_map(
        functools.partial(on_device, sizes),
        mesh=mesh,
        in_specs=(spectrum, spectrum, brick, brick),
        out_specs=brick,
        check_vma=False,
    )


def solution(mesh):
    return build(mesh, X_CHIPS, (512, 512, 512))
```

```python
import functools
import math

import jax
import jax.numpy as jnp
import ml_dtypes
import numpy as np
from jax import lax
from jax.experimental import pallas as pl
from jax.experimental.pallas import tpu as pltpu
from jax.sharding import PartitionSpec as P

step_size = 0.5
tv_weight = 0.5
smoothing = 0.5
MESH = pl.DeviceIdType.MESH
X_CHIPS = 4


def halves(table):
    high = table.astype(ml_dtypes.bfloat16)
    low = (table - high.astype(np.float64)).astype(ml_dtypes.bfloat16)
    return np.stack([high, low])


def cos_sin(length, rows, columns):
    phases = (np.asarray(rows)[:, None] * np.asarray(columns)[None, :]) % length
    angles = phases * (2.0 * math.pi / length)
    factor = 1.0 / math.sqrt(length)
    return np.cos(angles) * factor, np.sin(angles) * factor


class Sizes:
    def __init__(self, mesh_sizes, x_chips, ny, nz, nx):
        self.gx, self.gy, self.gz = mesh_sizes
        self.ny, self.nz, self.nx = ny, nz, nx
        self.plane = self.gx * self.gy
        self.planes = nz // (self.plane * self.gz)
        self.chips = x_chips
        self.ring = self.plane // x_chips
        self.by, self.bz, self.bx = ny // self.gy, nz // self.gz, nx // self.gx
        self.rows = self.by // self.gz
        self.lines = 2 * nz


def make_tables(s):
    c, n = cos_sin(s.nx, range(s.nx), range(s.nx))
    table_x = halves(np.concatenate([c, n], axis=0))
    c, n = cos_sin(s.ny, range(s.ny), range(s.ny))
    table_y = halves(np.concatenate([c, n], axis=1))
    k, r, g, x = np.meshgrid(
        range(s.planes), range(s.ring), range(s.gz), range(s.chips), indexing="ij"
    )
    kz = (((r * s.chips + x) * s.gz + g) * s.planes + k).reshape(-1)
    c, n = cos_sin(s.nz, range(s.nz), kz)
    table_z = halves(np.stack([c, -n], axis=-1).reshape(s.nz, s.lines))
    return table_x, table_y, table_z


def split(x):
    high = x.astype(jnp.bfloat16)
    return high, (x - high.astype(jnp.float32)).astype(jnp.bfloat16)


def dot3(a_high, a_low, b_high, b_low):
    f32 = jnp.float32
    return (
        jnp.dot(a_high, b_high, preferred_element_type=f32)
        + jnp.dot(a_high, b_low, preferred_element_type=f32)
        + jnp.dot(a_low, b_high, preferred_element_type=f32)
    )


def kernel(
    s, sr, si, tx, ty_hbm, tz_hbm, volume_hbm, weights_hbm, out,
    mid, mine, blocks, pencils, lines, bricks,
    ty, tz, volume, weights, fluxes, faces, halos,
    face_x, halo_x, flux_face_x, flux_halo_x,
    send1, recv1, send2, recv2, send3, recv3, load, face_send, face_recv,
):
    late = [
        pltpu.make_async_copy(source, to, load.at[i])
        for i, (source, to) in enumerate(
            ((ty_hbm, ty), (volume_hbm, volume), (weights_hbm, weights), (tz_hbm, tz))
        )
    ]
    for copy in late:
        copy.start()
    gx, gy, gz = lax.axis_index("gx"), lax.axis_index("gy"), lax.axis_index("gz")
    here = gx * s.gy + gy
    ring, chip = here // s.chips, here % s.chips
    half = s.nx
    lanes = s.nx // 128
    tile_y = min(256, s.ny)
    chunk = min(128, s.ny)

    def place(index):
        return (index // s.gy, index % s.gy, gz)

    def beside(step):
        return (gx, gy, (gz + step) % s.gz)

    barrier = pltpu.get_barrier_semaphore()

    def greet(i, _):
        pl.semaphore_signal(barrier, inc=1, device_id=place((here + i) % s.plane), device_id_type=MESH)
        return 0

    def greet_beside(i, _):
        pl.semaphore_signal(barrier, inc=1, device_id=beside(i), device_id_type=MESH)
        return 0

    lax.fori_loop(1, s.plane, greet, 0)
    lax.fori_loop(1, s.gz, greet_beside, 0)

    def transform_x(k):
        def body(t, _):
            def plane_rows(ref):
                first = t * chunk * lanes * s.planes + k
                return jnp.concatenate(
                    [
                        ref[pl.ds(first + j * s.planes, chunk, stride=lanes * s.planes), :]
                        for j in range(lanes)
                    ],
                    axis=1,
                )

            re_high, re_low = split(plane_rows(sr))
            im_high, im_low = split(plane_rows(si))
            high = jnp.concatenate(
                [jnp.concatenate([re_high, -im_high], 1), jnp.concatenate([im_high, re_high], 1)], 0
            )
            low = jnp.concatenate(
                [jnp.concatenate([re_low, -im_low], 1), jnp.concatenate([im_low, re_low], 1)], 0
            )
            both = dot3(high, low, tx[0], tx[1])
            re_high, re_low = split(both[:chunk])
            im_high, im_low = split(both[chunk:])
            at = pl.multiple_of(t * chunk, chunk)
            mid[0, pl.ds(at, chunk), :] = im_high
            mid[1, pl.ds(at, chunk), :] = im_low
            mid[0, pl.ds(s.ny + at, chunk), :] = re_high
            mid[1, pl.ds(s.ny + at, chunk), :] = re_low
            mid[0, pl.ds(2 * s.ny + at, chunk), :] = -im_high
            mid[1, pl.ds(2 * s.ny + at, chunk), :] = -im_low
            return 0

        lax.fori_loop(0, s.ny // chunk, body, 0)

    def transform_y(k):
        per = tile_y // s.by

        def body(t, _):
            at = pl.multiple_of(t * tile_y, tile_y)
            high, low = ty[0, pl.ds(at, tile_y), :], ty[1, pl.ds(at, tile_y), :]
            for c, first in ((0, s.ny), (1, 0)):
                o = dot3(
                    high, low, mid[0, first : first + 2 * s.ny, :], mid[1, first : first + 2 * s.ny, :]
                )
                for q in range(s.gx):
                    mine[pl.ds(q * s.gy + t * per, per), k, c] = o[
                        :, q * 128 : (q + 1) * 128
                    ].reshape(per, s.by, 128)
            return 0

        lax.fori_loop(0, s.ny // tile_y, body, 0)

    turns = []
    for h in range(1, s.ring // 2 + 1):
        turns += [h] if 2 * h == s.ring else [h, s.ring - h]

    def send_block(k, turn, dx):
        to = ((ring + turn) % s.ring) * s.chips + (chip + dx) % s.chips
        pltpu.make_async_remote_copy(
            src_ref=mine.at[to, k],
            dst_ref=blocks.at[k, pl.ds(2 * here, 2)],
            send_sem=send1,
            recv_sem=recv1.at[k, ring],
            device_id=place(to),
            device_id_type=MESH,
        ).start()

    before_x, after_x = (gx + s.gx - 1) % s.gx, (gx + 1) % s.gx
    before_y, after_y = (gy + s.gy - 1) % s.gy, (gy + 1) % s.gy
    flat = s.by * s.bz
    row_8 = lax.broadcasted_iota(jnp.int32, (8, 128), 0)
    lane_8 = lax.broadcasted_iota(jnp.int32, (8, 128), 1)
    lane = lax.broadcasted_iota(jnp.int32, (s.bz, 128), 1)
    row = lax.broadcasted_iota(jnp.int32, (s.bz, 128), 0)

    def take_lane(ref, which, to):
        pick = jnp.where(lane_8 == which, 1.0, 0.0)
        to[...] = lax.dot_general(
            pick,
            ref[...].reshape(flat, 128),
            (((1,), (1,)), ((), ())),
            precision=lax.Precision.HIGHEST,
            preferred_element_type=jnp.float32,
        )[:1]

    def put_lane(ref, which, to):
        pick = jnp.where((lane_8 == which) & (row_8 == 0), 1.0, 0.0)
        to[...] = lax.dot_general(
            jnp.broadcast_to(ref[...], (8, flat)),
            pick,
            (((0,), (0,)), ((), ())),
            precision=lax.Precision.HIGHEST,
            preferred_element_type=jnp.float32,
        ).reshape(s.by, s.bz, 128)

    def face_copies(stage, x_from, x_to, to_x, to_y, to_z):
        pairs = (
            (x_from, x_to, (to_x, gy, gz)),
            (faces.at[stage, 0], halos.at[stage, 0], (gx, to_y, gz)),
            (faces.at[stage, 1], halos.at[stage, 1], (gx, gy, to_z)),
        )
        return [
            pltpu.make_async_remote_copy(
                src_ref=source,
                dst_ref=target,
                send_sem=face_send.at[stage, i],
                recv_sem=face_recv.at[stage, i],
                device_id=to,
                device_id_type=MESH,
            )
            for i, (source, target, to) in enumerate(pairs)
        ]

    volume_faces = face_copies(0, face_x, halo_x, before_x, before_y, (gz + s.gz - 1) % s.gz)
    flux_faces = face_copies(1, flux_face_x, flux_halo_x, after_x, after_y, (gz + 1) % s.gz)

    def send_faces():
        take_lane(volume, 0, face_x)
        faces[0, 0, : s.bz] = volume[0]
        faces[0, 1, : s.by] = volume[:, 0, :]
        for copy in volume_faces:
            copy.start()

    def take_faces():
        for copy in volume_faces:
            copy.wait()
        put_lane(halo_x, 127, fluxes)

    def fluxes_inside():
        def one(y, v, ahead, x_halo, previous):
            ahead_z = jnp.where(
                row == s.bz - 1, halos[0, 1, pl.ds(y, 1), :], pltpu.roll(v, s.bz - 1, 0)
            )
            ahead_x = jnp.where(lane == 127, x_halo, pltpu.roll(v, 127, 1))
            slope_y = ahead - v
            slope_z = jnp.where((row == s.bz - 1) & (gz == s.gz - 1), 0.0, ahead_z - v)
            slope_x = jnp.where((lane == 127) & (gx == s.gx - 1), 0.0, ahead_x - v)
            squares = slope_y * slope_y + slope_z * slope_z + slope_x * slope_x + smoothing
            scaled = weights[y] * lax.rsqrt(squares)
            flux_y, flux_z, flux_x = scaled * slope_y, scaled * slope_z, scaled * slope_x
            gradient = previous - flux_y
            gradient = gradient + jnp.where(row == 0, 0.0, pltpu.roll(flux_z, 1, 0)) - flux_z
            gradient = gradient + jnp.where(lane == 0, 0.0, pltpu.roll(flux_x, 1, 1)) - flux_x
            fluxes[y] = flux_x
            faces[1, 1, pl.ds(y, 1), :] = flux_z[s.bz - 1 :]
            out[y] = v - (step_size * tv_weight) * gradient
            return flux_y

        last = s.by - 1
        previous = lax.fori_loop(
            0,
            last,
            lambda y, before: one(y, volume[y], volume[y + 1], fluxes[y], before),
            jnp.zeros((s.bz, 128), jnp.float32),
        )
        v = volume[last]
        ahead = jnp.where(gy == s.gy - 1, v, halos[0, 0, : s.bz])
        faces[1, 0, : s.bz] = one(last, v, ahead, fluxes[last], previous)

    def send_fluxes():
        take_lane(fluxes, 127, flux_face_x)
        for copy in flux_faces:
            copy.start()

    def take_fluxes():
        for copy in flux_faces:
            copy.wait()
        scale = step_size * tv_weight
        put_lane(flux_halo_x, 0, fluxes)
        out[...] = out[...] - jnp.where(gx == 0, 0.0, scale) * fluxes[...]
        out[0] = out[0] - jnp.where(gy == 0, 0.0, scale) * halos[1, 0, : s.bz]
        out[:, 0, :] = out[:, 0, :] - jnp.where(gz == 0, 0.0, scale) * halos[1, 1, : s.by]

    def plane(k, _):
        transform_x(k)

        @pl.when(k == 0)
        def _():
            late[0].wait()

        transform_y(k)

        @pl.when(k == 0)
        def _():
            pl.semaphore_wait(barrier, s.plane - 1 + s.gz - 1)

        for turn in turns:
            lax.fori_loop(0, s.chips, lambda dx, _: (send_block(k, turn, dx), 0)[1], 0)
        lax.fori_loop(1, s.chips, lambda dx, _: (send_block(k, 0, dx), 0)[1], 0)
        pltpu.make_async_copy(
            mine.at[here, k], blocks.at[k, pl.ds(2 * here, 2)], recv1.at[k, ring]
        ).start()

        @pl.when(k == 0)
        def _():
            late[1].wait()
            send_faces()

        return 0

    lax.fori_loop(0, s.planes, plane, 0)

    width = 2 * s.chips

    def forward(k, _):
        for turn in turns + [0]:
            source = (ring + s.ring - turn) % s.ring
            group = blocks.at[k, pl.ds(source * width, width)]
            pltpu.make_async_copy(group, group, recv1.at[k, source]).wait()

            def step(i, _):
                to = (gz + i) % s.gz
                pltpu.make_async_remote_copy(
                    src_ref=group.at[:, pl.ds(to * s.rows, s.rows), :],
                    dst_ref=pencils.at[pl.ds(((k * s.ring + source) * s.gz + gz) * width, width)],
                    send_sem=send2,
                    recv_sem=recv2,
                    device_id=beside(i),
                    device_id_type=MESH,
                ).start()
                return 0

            lax.fori_loop(1, s.gz, step, 0)
            pltpu.make_async_copy(
                group.at[:, pl.ds(gz * s.rows, s.rows), :],
                pencils.at[pl.ds(((k * s.ring + source) * s.gz + gz) * width, width)],
                recv2,
            ).start()
        return 0

    for k in range(s.planes):
        if k == s.planes - 1:
            late[2].wait()
            take_faces()
            fluxes_inside()
            send_fluxes()
        forward(k, 0)
    late[3].wait()
    pltpu.make_async_copy(pencils, pencils, recv2).wait()

    tile_z = min(256, s.nz)

    def transform_z(pair, _):
        pieces = [
            split(pencils[:, 2 * pair + j, :]) for j in range(2)
        ]
        high = jnp.concatenate([p[0] for p in pieces], axis=1)
        low = jnp.concatenate([p[1] for p in pieces], axis=1)
        for t in range(s.nz // tile_z):
            at = slice(t * tile_z, (t + 1) * tile_z)
            o = dot3(tz[0, at, :], tz[1, at, :], high, low)
            for j in range(2):
                lines[2 * pair + j, at, :] = o[:, j * 128 : (j + 1) * 128]

        def step(i, _):
            to = (gz + i) % s.gz
            pltpu.make_async_remote_copy(
                src_ref=lines.at[pl.ds(2 * pair, 2), pl.ds(to * s.bz, s.bz), :],
                dst_ref=bricks.at[gz, pl.ds(2 * pair, 2)],
                send_sem=send3,
                recv_sem=recv3,
                device_id=beside(i),
                device_id_type=MESH,
            ).start()
            return 0

        lax.fori_loop(1, s.gz, step, 0)
        pltpu.make_async_copy(
            lines.at[pl.ds(2 * pair, 2), pl.ds(gz * s.bz, s.bz), :],
            bricks.at[gz, pl.ds(2 * pair, 2)],
            recv3,
        ).start()
        return 0

    lax.fori_loop(0, s.rows // 2, transform_z, 0)
    take_fluxes()
    pltpu.make_async_copy(bricks, bricks, recv3).wait()
    out[...] = out[...] - step_size * bricks[...].reshape(out.shape)

    sent = mine.at[pl.ds(0, s.plane - 1)]
    pltpu.make_async_copy(sent, sent, send1).wait()
    sent = pencils.at[pl.ds(0, s.lines // s.gz * (s.gz - 1))]
    pltpu.make_async_copy(sent, sent, send2).wait()
    sent = bricks.at[pl.ds(0, s.gz - 1)]
    pltpu.make_async_copy(sent, sent, send3).wait()


def on_device(s, spectrum_real, spectrum_imag, volume, weights):
    tables = [jnp.asarray(t) for t in make_tables(s)]

    def rows(x):
        x = x.reshape(s.ny, s.planes, s.nx // 128, 128)
        return x.transpose(0, 2, 1, 3).reshape(-1, 128)

    f32, bf16 = jnp.float32, jnp.bfloat16
    brick = (s.by, s.bz, s.bx)
    face = max(s.by, s.bz)
    dma = pltpu.SemaphoreType.DMA
    return pl.pallas_call(
        functools.partial(kernel, s),
        out_shape=jax.ShapeDtypeStruct(brick, f32),
        in_specs=[pl.BlockSpec(memory_space=pltpu.VMEM)] * 3
        + [pl.BlockSpec(memory_space=pl.ANY)] * 4,
        out_specs=pl.BlockSpec(memory_space=pltpu.VMEM),
        scratch_shapes=[
            pltpu.VMEM((2, 3 * s.ny, s.nx), bf16),
            pltpu.VMEM((s.plane, s.planes, 2, s.by, 128), f32),
            pltpu.VMEM((s.planes, 2 * s.plane, s.by, 128), f32),
            pltpu.VMEM((s.lines, s.rows, 128), f32),
            pltpu.VMEM((s.rows, s.nz, 128), f32),
            pltpu.VMEM((s.gz, s.rows, s.bz, 128), f32),
            pltpu.VMEM(tables[1].shape, bf16),
            pltpu.VMEM(tables[2].shape, bf16),
            pltpu.VMEM(brick, f32),
            pltpu.VMEM(brick, f32),
            pltpu.VMEM(brick, f32),
            pltpu.VMEM((2, 2, face, 128), f32),
            pltpu.VMEM((2, 2, face, 128), f32),
            pltpu.VMEM((1, s.by * s.bz), f32),
            pltpu.VMEM((1, s.by * s.bz), f32),
            pltpu.VMEM((1, s.by * s.bz), f32),
            pltpu.VMEM((1, s.by * s.bz), f32),
            dma,
            dma((s.planes, s.ring)),
            dma,
            dma,
            dma,
            dma,
            dma((4,)),
            dma((2, 3)),
            dma((2, 3)),
        ],
        compiler_params=pltpu.CompilerParams(
            collective_id=0, has_side_effects=True, vmem_limit_bytes=60 * 1024 * 1024
        ),
    )(rows(spectrum_real), rows(spectrum_imag), *tables, volume, weights)


def build(mesh, x_chips, shape):
    sizes = Sizes([mesh.shape[a] for a in ("gx", "gy", "gz")], x_chips, *shape)
    spectrum, brick = P(None, ("gx", "gy", "gz"), None), P("gy", "gz", "gx")
    return jax.shard_map(
        functools.partial(on_device, sizes),
        mesh=mesh,
        in_specs=(spectrum, spectrum, brick, brick),
        out_specs=brick,
        check_vma=False,
    )


def solution(mesh):
    return build(mesh, X_CHIPS, (512, 512, 512))
```

```python
import functools
import math

import jax
import jax.numpy as jnp
import ml_dtypes
import numpy as np
from jax import lax
from jax.experimental import pallas as pl
from jax.experimental.pallas import tpu as pltpu
from jax.sharding import PartitionSpec as P

step_size = 0.5
tv_weight = 0.5
smoothing = 0.5
MESH = pl.DeviceIdType.MESH
X_CHIPS = 4
CLASSES = 4


def halves(table):
    high = table.astype(ml_dtypes.bfloat16)
    low = (table - high.astype(np.float64)).astype(ml_dtypes.bfloat16)
    return np.stack([high, low])


def cos_sin(length, rows, columns):
    phases = (np.asarray(rows)[:, None] * np.asarray(columns)[None, :]) % length
    angles = phases * (2.0 * math.pi / length)
    factor = 1.0 / math.sqrt(length)
    return np.cos(angles) * factor, np.sin(angles) * factor


class Sizes:
    def __init__(self, mesh_sizes, x_chips, ny, nz, nx):
        self.gx, self.gy, self.gz = mesh_sizes
        self.ny, self.nz, self.nx = ny, nz, nx
        self.plane = self.gx * self.gy
        self.planes = nz // (self.plane * self.gz)
        self.chips = x_chips
        self.ring = self.plane // x_chips
        self.by, self.bz, self.bx = ny // self.gy, nz // self.gz, nx // self.gx
        self.classes = CLASSES
        self.class_y = ny // self.classes
        self.rows = self.by // (self.gz * self.classes)
        self.lines = 2 * nz


def make_tables(s):
    c, n = cos_sin(s.nx, range(s.nx), range(s.nx))
    table_x = halves(np.concatenate([c, n], axis=0))
    table_y = []
    for r in range(s.classes):
        c, n = cos_sin(s.ny, range(r, s.ny, s.classes), range(s.class_y))
        table_y.append(halves(np.concatenate([c, n], axis=1)))
    table_y = np.stack(table_y)
    r, g, k, x = np.meshgrid(
        range(s.ring), range(s.gz), range(s.planes), range(s.chips), indexing="ij"
    )
    kz = (((r * s.chips + x) * s.gz + g) * s.planes + k).reshape(-1)
    c, n = cos_sin(s.nz, range(s.nz), kz)
    table_z = halves(np.stack([c, -n], axis=-1).reshape(s.nz, s.lines))
    return table_x, table_y, table_z


def class_of(r, re, im):
    r = jnp.asarray(r, jnp.int32)
    if len(re) == 2:
        sign = (1 - 2 * r).astype(jnp.float32)
        return re[0] + sign * re[1], im[0] + sign * im[1]
    odd = r % 2
    pair = (1 - 2 * odd).astype(jnp.float32)
    sign = (1 - 2 * (r // 2)).astype(jnp.float32)
    even_sign, odd_sign = sign * (1 - odd).astype(jnp.float32), sign * odd.astype(jnp.float32)
    re_1, im_1 = re[1] + pair * re[3], im[1] + pair * im[3]
    re_0, im_0 = re[0] + pair * re[2], im[0] + pair * im[2]
    return re_0 + even_sign * re_1 - odd_sign * im_1, im_0 + even_sign * im_1 + odd_sign * re_1


def split(x):
    high = x.astype(jnp.bfloat16)
    return high, (x - high.astype(jnp.float32)).astype(jnp.bfloat16)


def dot3(a_high, a_low, b_high, b_low):
    f32 = jnp.float32
    return (
        jnp.dot(a_high, b_high, preferred_element_type=f32)
        + jnp.dot(a_high, b_low, preferred_element_type=f32)
        + jnp.dot(a_low, b_high, preferred_element_type=f32)
    )


def kernel(
    s, sr_hbm, si_hbm, tx_hbm, ty_hbm, tz_hbm, volume_hbm, weights_hbm, out,
    sr, si, tx, ty, tz, volume, weights,
    mine, blocks, pencils, lines, bricks, faces, halos,
    send1, recv1, send2, recv2, send3, recv3, load, face_send, face_recv,
):
    load_sr, load_si, load_ty, load_tx, load_volume, load_weights, load_tz = copies = [
        pltpu.make_async_copy(source, to, load.at[i])
        for i, (source, to) in enumerate(
            (
                (sr_hbm, sr),
                (si_hbm, si),
                (ty_hbm, ty),
                (tx_hbm, tx),
                (volume_hbm, volume.at[pl.ds(0, s.by)]),
                (weights_hbm, weights),
                (tz_hbm, tz),
            )
        )
    ]
    for copy in copies:
        copy.start()
    gx, gy, gz = lax.axis_index("gx"), lax.axis_index("gy"), lax.axis_index("gz")
    here = gx * s.gy + gy
    ring, chip = here // s.chips, here % s.chips
    lanes = s.nx // 128
    class_y = s.class_y

    def place(index):
        return (index // s.gy, index % s.gy, gz)

    def beside(step):
        return (gx, gy, (gz + step) % s.gz)

    barrier = pltpu.get_barrier_semaphore()

    def greet(i, _):
        pl.semaphore_signal(barrier, inc=1, device_id=place((here + i) % s.plane), device_id_type=MESH)
        return 0

    def greet_beside(i, _):
        pl.semaphore_signal(barrier, inc=1, device_id=beside(i), device_id_type=MESH)
        return 0

    lax.fori_loop(1, s.plane, greet, 0)
    lax.fori_loop(1, s.gz, greet_beside, 0)

    def transform(r, k):
        def quarters(ref):
            return [
                jnp.concatenate(
                    [
                        ref[q, pl.ds(k + j * s.planes, class_y, stride=lanes * s.planes), :]
                        for j in range(lanes)
                    ],
                    axis=1,
                )
                for q in range(s.classes)
            ]

        re, im = class_of(r, quarters(sr), quarters(si))
        re_high, re_low = split(re)
        im_high, im_low = split(im)
        y_high, y_low = ty[r, 0], ty[r, 1]
        real = dot3(
            y_high, y_low, jnp.concatenate([re_high, -im_high]), jnp.concatenate([re_low, -im_low])
        )
        imag = dot3(
            y_high, y_low, jnp.concatenate([im_high, re_high]), jnp.concatenate([im_low, re_low])
        )
        re_high, re_low = split(real)
        im_high, im_low = split(imag)
        high = jnp.concatenate(
            [jnp.concatenate([re_high, -im_high], 1), jnp.concatenate([im_high, re_high], 1)], 0
        )
        low = jnp.concatenate(
            [jnp.concatenate([re_low, -im_low], 1), jnp.concatenate([im_low, re_low], 1)], 0
        )
        both = dot3(high, low, tx[0], tx[1])
        for c in range(2):
            for q in range(s.gx):
                mine[r, q * s.gy : (q + 1) * s.gy, k, c] = both[
                    c * class_y : (c + 1) * class_y, q * 128 : (q + 1) * 128
                ].reshape(s.gy, s.gz, s.rows, 128)

    turns = []
    for h in range(1, s.ring // 2 + 1):
        turns += [h] if 2 * h == s.ring else [h, s.ring - h]

    def send_block(r, planes, turn, dx):
        to = ((ring + turn) % s.ring) * s.chips + (chip + dx) % s.chips
        pltpu.make_async_remote_copy(
            src_ref=mine.at[r, to, planes],
            dst_ref=blocks.at[r, planes, pl.ds(2 * here, 2)],
            send_sem=send1,
            recv_sem=recv1.at[r, ring],
            device_id=place(to),
            device_id_type=MESH,
        ).start()

    def send_class(r, first, planes):
        planes = pl.ds(first, planes)
        for turn in turns:
            lax.fori_loop(0, s.chips, lambda dx, _: (send_block(r, planes, turn, dx), 0)[1], 0)
        lax.fori_loop(1, s.chips, lambda dx, _: (send_block(r, planes, 0, dx), 0)[1], 0)
        pltpu.make_async_copy(
            mine.at[r, here, planes], blocks.at[r, planes, pl.ds(2 * here, 2)], recv1.at[r, ring]
        ).start()

    before_x, after_x = (gx + s.gx - 1) % s.gx, (gx + 1) % s.gx
    before_y, after_y = (gy + s.gy - 1) % s.gy, (gy + 1) % s.gy
    lane = lax.broadcasted_iota(jnp.int32, (s.bz, 128), 1)
    row = lax.broadcasted_iota(jnp.int32, (s.bz, 128), 0)
    unroll = 4

    def face_copies(stage, to_x, to_y, to_z):
        return [
            pltpu.make_async_remote_copy(
                src_ref=faces.at[stage, i],
                dst_ref=halos.at[stage, i],
                send_sem=face_send.at[stage, i],
                recv_sem=face_recv.at[stage, i],
                device_id=to,
                device_id_type=MESH,
            )
            for i, to in enumerate(((to_x, gy, gz), (gx, to_y, gz), (gx, gy, to_z)))
        ]

    volume_faces = face_copies(0, before_x, before_y, (gz + s.gz - 1) % s.gz)
    flux_faces = face_copies(1, after_x, after_y, (gz + 1) % s.gz)

    def send_faces():
        def step(i, face):
            for j in range(unroll):
                y = i * unroll + j
                face = jnp.where(lane == y, pltpu.roll(volume[y], y, 1), face)
            return face

        faces[0, 0, : s.bz] = lax.fori_loop(
            0, s.by // unroll, step, jnp.zeros((s.bz, 128), jnp.float32)
        )
        faces[0, 1, : s.bz] = volume[0]
        faces[0, 2, : s.by] = volume[: s.by, 0, :]
        for copy in volume_faces:
            copy.start()

    def fluxes_inside():
        for copy in volume_faces:
            copy.wait()
        volume[s.by] = jnp.where(gy == s.gy - 1, volume[s.by - 1], halos[0, 1, : s.bz])
        last_z = (row == s.bz - 1) & (gz == s.gz - 1)
        last_x = (lane == 127) & (gx == s.gx - 1)
        scale = step_size * tv_weight

        def one(y, before, face):
            v = volume[y]
            ahead_z = jnp.where(
                row == s.bz - 1, halos[0, 2, pl.ds(y, 1), :], pltpu.roll(v, s.bz - 1, 0)
            )
            ahead_x = jnp.where(
                lane == 127, pltpu.roll(halos[0, 0, : s.bz], 127 - y, 1), pltpu.roll(v, 127, 1)
            )
            slope_y = volume[y + 1] - v
            slope_z = jnp.where(last_z, 0.0, ahead_z - v)
            slope_x = jnp.where(last_x, 0.0, ahead_x - v)
            squares = slope_y * slope_y + slope_z * slope_z + slope_x * slope_x + smoothing
            scaled = weights[y] * lax.rsqrt(squares)
            flux_y, flux_z, flux_x = scaled * slope_y, scaled * slope_z, scaled * slope_x
            gradient = before - flux_y
            gradient = gradient + jnp.where(row == 0, 0.0, pltpu.roll(flux_z, 1, 0)) - flux_z
            gradient = gradient + jnp.where(lane == 0, 0.0, pltpu.roll(flux_x, 1, 1)) - flux_x
            faces[1, 2, pl.ds(y, 1), :] = flux_z[s.bz - 1 :]
            out[y] = v - scale * gradient
            return flux_y, jnp.where(lane == y, pltpu.roll(flux_x, y + 1, 1), face)

        def step(i, carry):
            for j in range(unroll):
                carry = one(i * unroll + j, *carry)
            return carry

        zero = jnp.zeros((s.bz, 128), jnp.float32)
        flux_y, face = lax.fori_loop(0, s.by // unroll, step, (zero, zero))
        faces[1, 0, : s.bz] = face
        faces[1, 1, : s.bz] = flux_y
        for copy in flux_faces:
            copy.start()

    def take_fluxes():
        scale = step_size * tv_weight
        for copy in flux_faces:
            copy.wait()
        out[0] = out[0] - jnp.where(gy == 0, 0.0, scale) * halos[1, 1, : s.bz]

    def first_classes(k, _):
        @pl.when(k == 0)
        def _():
            for copy in (load_sr, load_si, load_ty, load_tx):
                copy.wait()

        transform(0, k)

        @pl.when(k == 0)
        def _():
            pl.semaphore_wait(barrier, s.plane - 1 + s.gz - 1)

        send_class(0, k, 1)

        @pl.when(k == 0)
        def _():
            load_volume.wait()
            send_faces()

        return 0

    def transform_class(r):
        lax.fori_loop(0, s.planes, lambda k, _: (transform(r, k), 0)[1], 0)

    lax.fori_loop(0, s.planes, first_classes, 0)
    for later in range(1, s.classes):
        transform_class(later)
        send_class(later, 0, s.planes)

    width = 2 * s.chips

    def forward(r):
        for position, turn in enumerate(turns + [0]):
            source = (ring + s.ring - turn) % s.ring
            group = blocks.at[r, :, pl.ds(source * width, width)]
            pltpu.make_async_copy(group, group, recv1.at[r, source]).wait()

            def step(i, _):
                pltpu.make_async_remote_copy(
                    src_ref=blocks.at[r, :, pl.ds(source * width, width), (gz + i) % s.gz],
                    dst_ref=pencils.at[r, source, gz],
                    send_sem=send2,
                    recv_sem=recv2.at[r],
                    device_id=beside(i),
                    device_id_type=MESH,
                ).start()
                return 0

            lax.fori_loop(1, s.gz, step, 0)
            pltpu.make_async_copy(
                blocks.at[r, :, pl.ds(source * width, width), gz],
                pencils.at[r, source, gz],
                recv2.at[r],
            ).start()

    tile_z = min(256, s.nz)

    def transform_z(r, first):
        pieces = [
            split(pencils[r, :, :, :, :, first + j, :].reshape(s.lines, 128)) for j in range(2)
        ]
        high = jnp.concatenate([p[0] for p in pieces], axis=1)
        low = jnp.concatenate([p[1] for p in pieces], axis=1)
        for t in range(s.nz // tile_z):
            at = slice(t * tile_z, (t + 1) * tile_z)
            o = dot3(tz[0, at, :], tz[1, at, :], high, low)
            for j in range(2):
                lines[r, first + j, at, :] = o[:, j * 128 : (j + 1) * 128]

        def step(i, _):
            to = (gz + i) % s.gz
            pltpu.make_async_remote_copy(
                src_ref=lines.at[r, pl.ds(first, 2), pl.ds(to * s.bz, s.bz), :],
                dst_ref=bricks.at[r, gz, pl.ds(first, 2)],
                send_sem=send3,
                recv_sem=recv3.at[r],
                device_id=beside(i),
                device_id_type=MESH,
            ).start()
            return 0

        lax.fori_loop(1, s.gz, step, 0)
        pltpu.make_async_copy(
            lines.at[r, pl.ds(first, 2), pl.ds(gz * s.bz, s.bz), :],
            bricks.at[r, gz, pl.ds(first, 2)],
            recv3.at[r],
        ).start()

    def finish_class(r):
        pltpu.make_async_copy(bricks.at[r], bricks.at[r], recv3.at[r]).wait()

        def one_row(m, _):
            y = m * s.classes + r
            x_flux = pltpu.roll(halos[1, 0, : s.bz], (128 - y) % 128, 1)
            outer = jnp.where((lane == 0) & (gx > 0), x_flux, 0.0) + jnp.where(
                (row == 0) & (gz > 0), halos[1, 2, pl.ds(y, 1), :], 0.0
            )
            data = bricks[r, m // s.rows, m % s.rows]
            out[y] = out[y] - step_size * (data + tv_weight * outer)
            return 0

        lax.fori_loop(0, s.gz * s.rows, one_row, 0)

    def gather_class(r, _):
        forward(r)

        @pl.when(r == 0)
        def _():
            load_tz.wait()

        pltpu.make_async_copy(pencils.at[r], pencils.at[r], recv2.at[r]).wait()
        for first in range(0, s.rows, 2):
            transform_z(r, first)

        @pl.when(r == 0)
        def _():
            load_weights.wait()
            fluxes_inside()

        return 0

    lax.fori_loop(0, s.classes, gather_class, 0)
    take_fluxes()
    lax.fori_loop(0, s.classes, lambda r, _: (finish_class(r), 0)[1], 0)

    sent = mine.at[:, pl.ds(0, s.plane - 1)]
    pltpu.make_async_copy(sent, sent, send1).wait()
    sent = pencils.at[:, :, pl.ds(0, s.gz - 1)]
    pltpu.make_async_copy(sent, sent, send2).wait()
    sent = bricks.at[:, pl.ds(0, s.gz - 1)]
    pltpu.make_async_copy(sent, sent, send3).wait()


def on_device(s, spectrum_real, spectrum_imag, volume, weights):
    tables = [jnp.asarray(t) for t in make_tables(s)]

    def rows(x):
        x = x.reshape(s.ny, s.planes, s.nx // 128, 128)
        return x.transpose(0, 2, 1, 3).reshape(s.classes, -1, 128)

    f32, bf16 = jnp.float32, jnp.bfloat16
    brick = (s.by, s.bz, s.bx)
    spectrum = (s.classes, s.class_y * s.planes * s.nx // 128, 128)
    face = max(s.by, s.bz)
    dma = pltpu.SemaphoreType.DMA
    return pl.pallas_call(
        functools.partial(kernel, s),
        out_shape=jax.ShapeDtypeStruct(brick, f32),
        in_specs=[pl.BlockSpec(memory_space=pl.ANY)] * 7,
        out_specs=pl.BlockSpec(memory_space=pltpu.VMEM),
        scratch_shapes=[
            pltpu.VMEM(spectrum, f32),
            pltpu.VMEM(spectrum, f32),
            *(pltpu.VMEM(table.shape, bf16) for table in tables),
            pltpu.VMEM((s.by + 1, s.bz, s.bx), f32),
            pltpu.VMEM(brick, f32),
            pltpu.VMEM((s.classes, s.plane, s.planes, 2, s.gz, s.rows, 128), f32),
            pltpu.VMEM((s.classes, s.planes, 2 * s.plane, s.gz, s.rows, 128), f32),
            pltpu.VMEM((s.classes, s.ring, s.gz, s.planes, 2 * s.chips, s.rows, 128), f32),
            pltpu.VMEM((s.classes, s.rows, s.nz, 128), f32),
            pltpu.VMEM((s.classes, s.gz, s.rows, s.bz, 128), f32),
            pltpu.VMEM((2, 3, face, 128), f32),
            pltpu.VMEM((2, 3, face, 128), f32),
            dma,
            dma((s.classes, s.ring)),
            dma,
            dma((s.classes,)),
            dma,
            dma((s.classes,)),
            dma((7,)),
            dma((2, 3)),
            dma((2, 3)),
        ],
        compiler_params=pltpu.CompilerParams(
            collective_id=0, has_side_effects=True, vmem_limit_bytes=62 * 1024 * 1024
        ),
    )(rows(spectrum_real), rows(spectrum_imag), *tables, volume, weights)


def build(mesh, x_chips, shape):
    sizes = Sizes([mesh.shape[a] for a in ("gx", "gy", "gz")], x_chips, *shape)
    spectrum, brick = P(None, ("gx", "gy", "gz"), None), P("gy", "gz", "gx")
    return jax.shard_map(
        functools.partial(on_device, sizes),
        mesh=mesh,
        in_specs=(spectrum, spectrum, brick, brick),
        out_specs=brick,
        check_vma=False,
    )


def solution(mesh):
    return build(mesh, X_CHIPS, (512, 512, 512))
```

```python
import functools
import math

import jax
import jax.numpy as jnp
import ml_dtypes
import numpy as np
from jax import lax
from jax.experimental import pallas as pl
from jax.experimental.pallas import tpu as pltpu
from jax.sharding import PartitionSpec as P

step_size = 0.5
tv_weight = 0.5
smoothing = 0.5
MESH = pl.DeviceIdType.MESH
X_CHIPS = 4
CLASSES = 4
DELIVERIES = 8


def halves(table):
    high = table.astype(ml_dtypes.bfloat16)
    low = (table - high.astype(np.float64)).astype(ml_dtypes.bfloat16)
    return np.stack([high, low])


def cos_sin(length, rows, columns):
    phases = (np.asarray(rows)[:, None] * np.asarray(columns)[None, :]) % length
    angles = phases * (2.0 * math.pi / length)
    factor = 1.0 / math.sqrt(length)
    return np.cos(angles) * factor, np.sin(angles) * factor


class Sizes:
    def __init__(self, mesh_sizes, x_chips, ny, nz, nx):
        self.gx, self.gy, self.gz = mesh_sizes
        self.ny, self.nz, self.nx = ny, nz, nx
        self.plane = self.gx * self.gy
        self.planes = nz // (self.plane * self.gz)
        self.chips = x_chips
        self.ring = self.plane // x_chips
        self.by, self.bz, self.bx = ny // self.gy, nz // self.gz, nx // self.gx
        self.classes = CLASSES
        self.class_y = ny // self.classes
        self.rows = self.by // (self.gz * self.classes)
        self.lines = 2 * nz


def make_tables(s):
    c, n = cos_sin(s.nx, range(s.nx), range(s.nx))
    table_x = halves(np.concatenate([c, n], axis=0))
    table_y = []
    for r in range(s.classes):
        c, n = cos_sin(s.ny, range(r, s.ny, s.classes), range(s.class_y))
        table_y.append(halves(np.concatenate([c, n], axis=1)))
    table_y = np.stack(table_y)
    r, g, k, x = np.meshgrid(
        range(s.ring), range(s.gz), range(s.planes), range(s.chips), indexing="ij"
    )
    kz = (((r * s.chips + x) * s.gz + g) * s.planes + k).reshape(-1)
    c, n = cos_sin(s.nz, range(s.nz), kz)
    table_z = halves(np.stack([c, -n], axis=-1).reshape(s.nz, s.lines))
    return table_x, table_y, table_z


def class_of(r, re, im):
    r = jnp.asarray(r, jnp.int32)
    if len(re) == 2:
        sign = (1 - 2 * r).astype(jnp.float32)
        return re[0] + sign * re[1], im[0] + sign * im[1]
    odd = r % 2
    pair = (1 - 2 * odd).astype(jnp.float32)
    sign = (1 - 2 * (r // 2)).astype(jnp.float32)
    even_sign, odd_sign = sign * (1 - odd).astype(jnp.float32), sign * odd.astype(jnp.float32)
    re_1, im_1 = re[1] + pair * re[3], im[1] + pair * im[3]
    re_0, im_0 = re[0] + pair * re[2], im[0] + pair * im[2]
    return re_0 + even_sign * re_1 - odd_sign * im_1, im_0 + even_sign * im_1 + odd_sign * re_1


def split(x):
    high = x.astype(jnp.bfloat16)
    return high, (x - high.astype(jnp.float32)).astype(jnp.bfloat16)


def dot3(a_high, a_low, b_high, b_low):
    f32 = jnp.float32
    return (
        jnp.dot(a_high, b_high, preferred_element_type=f32)
        + jnp.dot(a_high, b_low, preferred_element_type=f32)
        + jnp.dot(a_low, b_high, preferred_element_type=f32)
    )


def kernel(
    s, sr_hbm, si_hbm, tx_hbm, ty_hbm, tz_hbm, volume_hbm, weights_hbm, result,
    sr, si, tx, ty, tz, volume, weights,
    out, mine, blocks, pencils, lines, bricks, faces, halos,
    send1, recv1, send2, recv2, send3, recv3, load, store, face_send, face_recv,
):
    load_sr, load_si, load_ty, load_tx, load_volume, load_weights, load_tz = copies = [
        pltpu.make_async_copy(source, to, load.at[i])
        for i, (source, to) in enumerate(
            (
                (sr_hbm, sr),
                (si_hbm, si),
                (ty_hbm, ty),
                (tx_hbm, tx),
                (volume_hbm, volume.at[pl.ds(0, s.by)]),
                (weights_hbm, weights),
                (tz_hbm, tz),
            )
        )
    ]
    for copy in copies[:4]:
        copy.start()
    gx, gy, gz = lax.axis_index("gx"), lax.axis_index("gy"), lax.axis_index("gz")
    here = gx * s.gy + gy
    ring, chip = here // s.chips, here % s.chips
    lanes = s.nx // 128
    class_y = s.class_y

    def place(index):
        return (index // s.gy, index % s.gy, gz)

    def beside(step):
        return (gx, gy, (gz + step) % s.gz)

    barrier = pltpu.get_barrier_semaphore()

    def greet(i, _):
        pl.semaphore_signal(barrier, inc=1, device_id=place((here + i) % s.plane), device_id_type=MESH)
        return 0

    def greet_beside(i, _):
        pl.semaphore_signal(barrier, inc=1, device_id=beside(i), device_id_type=MESH)
        return 0

    lax.fori_loop(1, s.plane, greet, 0)
    lax.fori_loop(1, s.gz, greet_beside, 0)

    def transform(r, k):
        def quarters(ref):
            return [
                jnp.concatenate(
                    [
                        ref[q, pl.ds(k + j * s.planes, class_y, stride=lanes * s.planes), :]
                        for j in range(lanes)
                    ],
                    axis=1,
                )
                for q in range(s.classes)
            ]

        re, im = class_of(r, quarters(sr), quarters(si))
        re_high, re_low = split(re)
        im_high, im_low = split(im)
        y_high, y_low = ty[r, 0], ty[r, 1]
        real = dot3(
            y_high, y_low, jnp.concatenate([re_high, -im_high]), jnp.concatenate([re_low, -im_low])
        )
        imag = dot3(
            y_high, y_low, jnp.concatenate([im_high, re_high]), jnp.concatenate([im_low, re_low])
        )
        re_high, re_low = split(real)
        im_high, im_low = split(imag)
        high = jnp.concatenate(
            [jnp.concatenate([re_high, -im_high], 1), jnp.concatenate([im_high, re_high], 1)], 0
        )
        low = jnp.concatenate(
            [jnp.concatenate([re_low, -im_low], 1), jnp.concatenate([im_low, re_low], 1)], 0
        )
        both = dot3(high, low, tx[0], tx[1])
        for c in range(2):
            for q in range(s.gx):
                mine[r, q * s.gy : (q + 1) * s.gy, k, c] = both[
                    c * class_y : (c + 1) * class_y, q * 128 : (q + 1) * 128
                ].reshape(s.gy, s.gz, s.rows, 128)

    turns = []
    for h in range(1, s.ring // 2 + 1):
        turns += [h] if 2 * h == s.ring else [h, s.ring - h]

    def send_block(r, planes, turn, dx):
        to = ((ring + turn) % s.ring) * s.chips + (chip + dx) % s.chips
        pltpu.make_async_remote_copy(
            src_ref=mine.at[r, to, planes],
            dst_ref=blocks.at[r, planes, pl.ds(2 * here, 2)],
            send_sem=send1,
            recv_sem=recv1.at[r, ring],
            device_id=place(to),
            device_id_type=MESH,
        ).start()

    def send_class(r, first, planes):
        planes = pl.ds(first, planes)
        for turn in turns:
            lax.fori_loop(0, s.chips, lambda dx, _: (send_block(r, planes, turn, dx), 0)[1], 0)
        lax.fori_loop(1, s.chips, lambda dx, _: (send_block(r, planes, 0, dx), 0)[1], 0)
        pltpu.make_async_copy(
            mine.at[r, here, planes], blocks.at[r, planes, pl.ds(2 * here, 2)], recv1.at[r, ring]
        ).start()

    before_x, after_x = (gx + s.gx - 1) % s.gx, (gx + 1) % s.gx
    before_y, after_y = (gy + s.gy - 1) % s.gy, (gy + 1) % s.gy
    lane = lax.broadcasted_iota(jnp.int32, (s.bz, 128), 1)
    row = lax.broadcasted_iota(jnp.int32, (s.bz, 128), 0)
    unroll = 4

    def face_copies(stage, to_x, to_y, to_z):
        return [
            pltpu.make_async_remote_copy(
                src_ref=faces.at[stage, i],
                dst_ref=halos.at[stage, i],
                send_sem=face_send.at[stage, i],
                recv_sem=face_recv.at[stage, i],
                device_id=to,
                device_id_type=MESH,
            )
            for i, to in enumerate(((to_x, gy, gz), (gx, to_y, gz), (gx, gy, to_z)))
        ]

    volume_faces = face_copies(0, before_x, before_y, (gz + s.gz - 1) % s.gz)
    flux_faces = face_copies(1, after_x, after_y, (gz + 1) % s.gz)

    def send_faces():
        def step(i, face):
            for j in range(unroll):
                y = i * unroll + j
                face = jnp.where(lane == y, pltpu.roll(volume[y], y, 1), face)
            return face

        faces[0, 0, : s.bz] = lax.fori_loop(
            0, s.by // unroll, step, jnp.zeros((s.bz, 128), jnp.float32)
        )
        faces[0, 1, : s.bz] = volume[0]
        faces[0, 2, : s.by] = volume[: s.by, 0, :]
        for copy in volume_faces:
            copy.start()

    def fluxes_inside():
        for copy in volume_faces:
            copy.wait()
        volume[s.by] = jnp.where(gy == s.gy - 1, volume[s.by - 1], halos[0, 1, : s.bz])
        last_z = (row == s.bz - 1) & (gz == s.gz - 1)
        last_x = (lane == 127) & (gx == s.gx - 1)
        scale = step_size * tv_weight

        def one(y, before, face):
            v = volume[y]
            ahead_z = jnp.where(
                row == s.bz - 1, halos[0, 2, pl.ds(y, 1), :], pltpu.roll(v, s.bz - 1, 0)
            )
            ahead_x = jnp.where(
                lane == 127, pltpu.roll(halos[0, 0, : s.bz], 127 - y, 1), pltpu.roll(v, 127, 1)
            )
            slope_y = volume[y + 1] - v
            slope_z = jnp.where(last_z, 0.0, ahead_z - v)
            slope_x = jnp.where(last_x, 0.0, ahead_x - v)
            squares = slope_y * slope_y + slope_z * slope_z + slope_x * slope_x + smoothing
            scaled = weights[y] * lax.rsqrt(squares)
            flux_y, flux_z, flux_x = scaled * slope_y, scaled * slope_z, scaled * slope_x
            gradient = before - flux_y
            gradient = gradient + jnp.where(row == 0, 0.0, pltpu.roll(flux_z, 1, 0)) - flux_z
            gradient = gradient + jnp.where(lane == 0, 0.0, pltpu.roll(flux_x, 1, 1)) - flux_x
            faces[1, 2, pl.ds(y, 1), :] = flux_z[s.bz - 1 :]
            out[y // s.classes, y % s.classes] = v - scale * gradient
            return flux_y, jnp.where(lane == y, pltpu.roll(flux_x, y + 1, 1), face)

        def step(i, carry):
            for j in range(unroll):
                carry = one(i * unroll + j, *carry)
            return carry

        zero = jnp.zeros((s.bz, 128), jnp.float32)
        flux_y, face = lax.fori_loop(0, s.by // unroll, step, (zero, zero))
        faces[1, 0, : s.bz] = face
        faces[1, 1, : s.bz] = flux_y
        for copy in flux_faces:
            copy.start()

    def take_fluxes():
        scale = step_size * tv_weight
        for copy in flux_faces:
            copy.wait()
        out[0, 0] = out[0, 0] - jnp.where(gy == 0, 0.0, scale) * halos[1, 1, : s.bz]

    def first_classes(k, _):
        @pl.when(k == 0)
        def _():
            for copy in (load_sr, load_si, load_ty, load_tx):
                copy.wait()

        transform(0, k)

        @pl.when(k == 0)
        def _():
            pl.semaphore_wait(barrier, s.plane - 1 + s.gz - 1)

        send_class(0, k, 1)

        @pl.when(k == 0)
        def _():
            for copy in copies[4:]:
                copy.start()
            load_volume.wait()
            send_faces()

        return 0

    def transform_class(r):
        lax.fori_loop(0, s.planes, lambda k, _: (transform(r, k), 0)[1], 0)

    lax.fori_loop(0, s.planes, first_classes, 0)
    for later in range(1, s.classes):
        transform_class(later)
        send_class(later, 0, s.planes)

    width = 2 * s.chips

    def forward(r):
        for position, turn in enumerate(turns + [0]):
            source = (ring + s.ring - turn) % s.ring
            group = blocks.at[r, :, pl.ds(source * width, width)]
            pltpu.make_async_copy(group, group, recv1.at[r, source]).wait()

            def step(i, _):
                pltpu.make_async_remote_copy(
                    src_ref=blocks.at[r, :, pl.ds(source * width, width), (gz + i) % s.gz],
                    dst_ref=pencils.at[r, source, gz],
                    send_sem=send2,
                    recv_sem=recv2.at[r],
                    device_id=beside(i),
                    device_id_type=MESH,
                ).start()
                return 0

            lax.fori_loop(1, s.gz, step, 0)
            pltpu.make_async_copy(
                blocks.at[r, :, pl.ds(source * width, width), gz],
                pencils.at[r, source, gz],
                recv2.at[r],
            ).start()

    tile_z = min(256, s.nz)

    def transform_z(r, first):
        pieces = [
            split(pencils[r, :, :, :, :, first + j, :].reshape(s.lines, 128)) for j in range(2)
        ]
        high = jnp.concatenate([p[0] for p in pieces], axis=1)
        low = jnp.concatenate([p[1] for p in pieces], axis=1)
        for t in range(s.nz // tile_z):
            at = slice(t * tile_z, (t + 1) * tile_z)
            o = dot3(tz[0, at, :], tz[1, at, :], high, low)
            for j in range(2):
                lines[r, first + j, at, :] = o[:, j * 128 : (j + 1) * 128]

        def step(i, _):
            to = (gz + i) % s.gz
            pltpu.make_async_remote_copy(
                src_ref=lines.at[r, pl.ds(first, 2), pl.ds(to * s.bz, s.bz), :],
                dst_ref=bricks.at[r, gz, pl.ds(first, 2)],
                send_sem=send3,
                recv_sem=recv3.at[r],
                device_id=beside(i),
                device_id_type=MESH,
            ).start()
            return 0

        lax.fori_loop(1, s.gz, step, 0)
        pltpu.make_async_copy(
            lines.at[r, pl.ds(first, 2), pl.ds(gz * s.bz, s.bz), :],
            bricks.at[r, gz, pl.ds(first, 2)],
            recv3.at[r],
        ).start()

    def store_class(r):
        return pltpu.make_async_copy(out.at[:, r], result.at[:, r], store.at[r])

    def finish_class(r):
        pltpu.make_async_copy(bricks.at[r], bricks.at[r], recv3.at[r]).wait()

        def some_rows(i, _):
            for j in range(unroll):
                m = i * unroll + j
                y = m * s.classes + r
                x_flux = pltpu.roll(halos[1, 0, : s.bz], (128 - y) % 128, 1)
                outer = jnp.where((lane == 0) & (gx > 0), x_flux, 0.0) + jnp.where(
                    (row == 0) & (gz > 0), halos[1, 2, pl.ds(y, 1), :], 0.0
                )
                data = bricks[r, m // s.rows, m % s.rows]
                out[m, r] = out[m, r] - step_size * (data + tv_weight * outer)
            return 0

        lax.fori_loop(0, s.gz * s.rows // unroll, some_rows, 0)
        store_class(r).start()

    def gather_class(r, _):
        forward(r)

        @pl.when(r == 0)
        def _():
            load_tz.wait()

        pltpu.make_async_copy(pencils.at[r], pencils.at[r], recv2.at[r]).wait()
        for first in range(0, s.rows, 2):
            transform_z(r, first)

        @pl.when(r == 0)
        def _():
            load_weights.wait()
            fluxes_inside()

        @pl.when(r == s.classes - 1)
        def _():
            take_fluxes()
            for ready in range(s.classes - 1):
                finish_class(ready)

        return 0

    lax.fori_loop(0, s.classes, gather_class, 0)
    finish_class(s.classes - 1)
    for ready in range(s.classes):
        store_class(ready).wait()

    sent = mine.at[:, pl.ds(0, s.plane - 1)]
    pltpu.make_async_copy(sent, sent, send1).wait()
    sent = pencils.at[:, :, pl.ds(0, s.gz - 1)]
    pltpu.make_async_copy(sent, sent, send2).wait()
    sent = bricks.at[:, pl.ds(0, s.gz - 1)]
    pltpu.make_async_copy(sent, sent, send3).wait()


def deliver_kernel(source, to, held, taken, done):
    rows = source.shape[0] // DELIVERIES
    parts = [pl.ds(i * rows, rows) for i in range(DELIVERIES)]
    take = [
        pltpu.make_async_copy(source.at[part], held.at[part], taken.at[i])
        for i, part in enumerate(parts)
    ]
    give = [
        pltpu.make_async_copy(held.at[part], to.at[part], done.at[i])
        for i, part in enumerate(parts)
    ]
    for copy in take:
        copy.start()
    for first, second in zip(take, give):
        first.wait()
        second.start()
    for copy in give:
        copy.wait()


def deliver(x):
    return pl.pallas_call(
        deliver_kernel,
        out_shape=jax.ShapeDtypeStruct(x.shape, x.dtype),
        in_specs=[pl.BlockSpec(memory_space=pl.ANY)],
        out_specs=pl.BlockSpec(memory_space=pl.ANY),
        scratch_shapes=[
            pltpu.VMEM(x.shape, x.dtype),
            pltpu.SemaphoreType.DMA((DELIVERIES,)),
            pltpu.SemaphoreType.DMA((DELIVERIES,)),
        ],
    )(x)


def on_device(s, spectrum_real, spectrum_imag, volume, weights):
    tables = [jnp.asarray(t) for t in make_tables(s)]

    def rows(x):
        x = x.reshape(s.ny, s.planes, s.nx // 128, 128)
        return x.transpose(0, 2, 1, 3).reshape(s.classes, -1, 128)

    f32, bf16 = jnp.float32, jnp.bfloat16
    brick = (s.by, s.bz, s.bx)
    classed = (s.by // s.classes, s.classes, s.bz, s.bx)
    spectrum = (s.classes, s.class_y * s.planes * s.nx // 128, 128)
    face = max(s.by, s.bz)
    dma = pltpu.SemaphoreType.DMA
    updated = pl.pallas_call(
        functools.partial(kernel, s),
        out_shape=jax.ShapeDtypeStruct(classed, f32),
        in_specs=[pl.BlockSpec(memory_space=pl.ANY)] * 7,
        out_specs=pl.BlockSpec(memory_space=pl.ANY),
        scratch_shapes=[
            pltpu.VMEM(spectrum, f32),
            pltpu.VMEM(spectrum, f32),
            *(pltpu.VMEM(table.shape, bf16) for table in tables),
            pltpu.VMEM((s.by + 1, s.bz, s.bx), f32),
            pltpu.VMEM(brick, f32),
            pltpu.VMEM(classed, f32),
            pltpu.VMEM((s.classes, s.plane, s.planes, 2, s.gz, s.rows, 128), f32),
            pltpu.VMEM((s.classes, s.planes, 2 * s.plane, s.gz, s.rows, 128), f32),
            pltpu.VMEM((s.classes, s.ring, s.gz, s.planes, 2 * s.chips, s.rows, 128), f32),
            pltpu.VMEM((s.classes, s.rows, s.nz, 128), f32),
            pltpu.VMEM((s.classes, s.gz, s.rows, s.bz, 128), f32),
            pltpu.VMEM((2, 3, face, 128), f32),
            pltpu.VMEM((2, 3, face, 128), f32),
            dma,
            dma((s.classes, s.ring)),
            dma,
            dma((s.classes,)),
            dma,
            dma((s.classes,)),
            dma((7,)),
            dma((s.classes,)),
            dma((2, 3)),
            dma((2, 3)),
        ],
        compiler_params=pltpu.CompilerParams(
            collective_id=0, has_side_effects=True, vmem_limit_bytes=62 * 1024 * 1024
        ),
    )(rows(spectrum_real), rows(spectrum_imag), *tables, volume, weights)
    return deliver(updated.reshape(brick))


def build(mesh, x_chips, shape):
    sizes = Sizes([mesh.shape[a] for a in ("gx", "gy", "gz")], x_chips, *shape)
    spectrum, brick = P(None, ("gx", "gy", "gz"), None), P("gy", "gz", "gx")
    return jax.shard_map(
        functools.partial(on_device, sizes),
        mesh=mesh,
        in_specs=(spectrum, spectrum, brick, brick),
        out_specs=brick,
        check_vma=False,
    )


def solution(mesh):
    return build(mesh, X_CHIPS, (512, 512, 512))
```

```python
import functools
import math

import jax
import jax.numpy as jnp
import ml_dtypes
import numpy as np
from jax import lax
from jax.experimental import pallas as pl
from jax.experimental.pallas import tpu as pltpu
from jax.sharding import PartitionSpec as P

step_size = 0.5
tv_weight = 0.5
smoothing = 0.5
MESH = pl.DeviceIdType.MESH
X_CHIPS = 4
CLASSES = 4
DELIVERIES = 8


def halves(table):
    high = table.astype(ml_dtypes.bfloat16)
    low = (table - high.astype(np.float64)).astype(ml_dtypes.bfloat16)
    return np.stack([high, low])


def cos_sin(length, rows, columns):
    phases = (np.asarray(rows)[:, None] * np.asarray(columns)[None, :]) % length
    angles = phases * (2.0 * math.pi / length)
    factor = 1.0 / math.sqrt(length)
    return np.cos(angles) * factor, np.sin(angles) * factor


class Sizes:
    def __init__(self, mesh_sizes, x_chips, ny, nz, nx):
        self.gx, self.gy, self.gz = mesh_sizes
        self.ny, self.nz, self.nx = ny, nz, nx
        self.plane = self.gx * self.gy
        self.planes = nz // (self.plane * self.gz)
        self.chips = x_chips
        self.ring = self.plane // x_chips
        self.by, self.bz, self.bx = ny // self.gy, nz // self.gz, nx // self.gx
        self.classes = CLASSES
        self.class_y = ny // self.classes
        self.rows = self.by // (self.gz * self.classes)
        self.lines = 2 * nz


def make_tables(s):
    c, n = cos_sin(s.nx, range(s.nx), range(s.nx))
    table_x = halves(np.concatenate([c, n], axis=0))
    table_y = []
    for r in range(s.classes):
        c, n = cos_sin(s.ny, range(r, s.ny, s.classes), range(s.class_y))
        table_y.append(halves(np.concatenate([c, n], axis=1)))
    table_y = np.stack(table_y)
    r, g, k, x = np.meshgrid(
        range(s.ring), range(s.gz), range(s.planes), range(s.chips), indexing="ij"
    )
    kz = (((r * s.chips + x) * s.gz + g) * s.planes + k).reshape(-1)
    c, n = cos_sin(s.nz, range(s.nz), kz)
    table_z = halves(np.stack([c, -n], axis=-1).reshape(s.nz, s.lines))
    return table_x, table_y, table_z


def class_of(r, re, im):
    r = jnp.asarray(r, jnp.int32)
    if len(re) == 2:
        sign = (1 - 2 * r).astype(jnp.float32)
        return re[0] + sign * re[1], im[0] + sign * im[1]
    odd = r % 2
    pair = (1 - 2 * odd).astype(jnp.float32)
    sign = (1 - 2 * (r // 2)).astype(jnp.float32)
    even_sign, odd_sign = sign * (1 - odd).astype(jnp.float32), sign * odd.astype(jnp.float32)
    re_1, im_1 = re[1] + pair * re[3], im[1] + pair * im[3]
    re_0, im_0 = re[0] + pair * re[2], im[0] + pair * im[2]
    return re_0 + even_sign * re_1 - odd_sign * im_1, im_0 + even_sign * im_1 + odd_sign * re_1


def split(x):
    high = x.astype(jnp.bfloat16)
    return high, (x - high.astype(jnp.float32)).astype(jnp.bfloat16)


def dot3(a_high, a_low, b_high, b_low):
    f32 = jnp.float32
    return (
        jnp.dot(a_high, b_high, preferred_element_type=f32)
        + jnp.dot(a_high, b_low, preferred_element_type=f32)
        + jnp.dot(a_low, b_high, preferred_element_type=f32)
    )


def kernel(
    s, sr_hbm, si_hbm, tx_hbm, ty_hbm, tz_hbm, volume_hbm, weights_hbm, result,
    sr, si, tx, ty, tz, volume, weights,
    out, mine, blocks, pencils, lines, bricks, faces, halos,
    send1, recv1, send2, recv2, send3, recv3, load, store, face_send, face_recv,
):
    load_sr, load_si, load_ty, load_tx, load_volume, load_weights, load_tz = copies = [
        pltpu.make_async_copy(source, to, load.at[i])
        for i, (source, to) in enumerate(
            (
                (sr_hbm, sr),
                (si_hbm, si),
                (ty_hbm, ty),
                (tx_hbm, tx),
                (volume_hbm, volume.at[pl.ds(0, s.by)]),
                (weights_hbm, weights),
                (tz_hbm, tz),
            )
        )
    ]
    for copy in copies[:4]:
        copy.start()
    gx, gy, gz = lax.axis_index("gx"), lax.axis_index("gy"), lax.axis_index("gz")
    here = gx * s.gy + gy
    ring, chip = here // s.chips, here % s.chips
    lanes = s.nx // 128
    class_y = s.class_y

    def place(index):
        return (index // s.gy, index % s.gy, gz)

    def beside(step):
        return (gx, gy, (gz + step) % s.gz)

    barrier = pltpu.get_barrier_semaphore()

    def greet(i, _):
        pl.semaphore_signal(barrier, inc=1, device_id=place((here + i) % s.plane), device_id_type=MESH)
        return 0

    def greet_beside(i, _):
        pl.semaphore_signal(barrier, inc=1, device_id=beside(i), device_id_type=MESH)
        return 0

    for i in range(1, s.plane):
        greet(i, 0)
    for i in range(1, s.gz):
        greet_beside(i, 0)

    def transform(r, k, before_x=None):
        def quarters(ref):
            return [
                jnp.concatenate(
                    [
                        ref[q, pl.ds(k + j * s.planes, class_y, stride=lanes * s.planes), :]
                        for j in range(lanes)
                    ],
                    axis=1,
                )
                for q in range(s.classes)
            ]

        re, im = class_of(r, quarters(sr), quarters(si))
        re_high, re_low = split(re)
        im_high, im_low = split(im)
        y_high, y_low = ty[r, 0], ty[r, 1]
        real = dot3(
            y_high, y_low, jnp.concatenate([re_high, -im_high]), jnp.concatenate([re_low, -im_low])
        )
        imag = dot3(
            y_high, y_low, jnp.concatenate([im_high, re_high]), jnp.concatenate([im_low, re_low])
        )
        if before_x is not None:
            before_x()
        re_high, re_low = split(real)
        im_high, im_low = split(imag)
        high = jnp.concatenate(
            [jnp.concatenate([re_high, -im_high], 1), jnp.concatenate([im_high, re_high], 1)], 0
        )
        low = jnp.concatenate(
            [jnp.concatenate([re_low, -im_low], 1), jnp.concatenate([im_low, re_low], 1)], 0
        )
        both = dot3(high, low, tx[0], tx[1])
        for c in range(2):
            for q in range(s.gx):
                mine[r, q * s.gy : (q + 1) * s.gy, k, c] = both[
                    c * class_y : (c + 1) * class_y, q * 128 : (q + 1) * 128
                ].reshape(s.gy, s.gz, s.rows, 128)

    turns = []
    for h in range(1, s.ring // 2 + 1):
        turns += [h] if 2 * h == s.ring else [h, s.ring - h]

    def send_block(r, planes, turn, dx):
        to = ((ring + turn) % s.ring) * s.chips + (chip + dx) % s.chips
        pltpu.make_async_remote_copy(
            src_ref=mine.at[r, to, planes],
            dst_ref=blocks.at[r, planes, pl.ds(2 * here, 2)],
            send_sem=send1,
            recv_sem=recv1.at[r, ring],
            device_id=place(to),
            device_id_type=MESH,
        ).start()

    def send_class(r, first, planes):
        planes = pl.ds(first, planes)
        for turn in turns:
            lax.fori_loop(0, s.chips, lambda dx, _: (send_block(r, planes, turn, dx), 0)[1], 0)
        lax.fori_loop(1, s.chips, lambda dx, _: (send_block(r, planes, 0, dx), 0)[1], 0)
        pltpu.make_async_copy(
            mine.at[r, here, planes], blocks.at[r, planes, pl.ds(2 * here, 2)], recv1.at[r, ring]
        ).start()

    before_x, after_x = (gx + s.gx - 1) % s.gx, (gx + 1) % s.gx
    before_y, after_y = (gy + s.gy - 1) % s.gy, (gy + 1) % s.gy
    lane = lax.broadcasted_iota(jnp.int32, (s.bz, 128), 1)
    row = lax.broadcasted_iota(jnp.int32, (s.bz, 128), 0)
    unroll = 4

    def face_copies(stage, to_x, to_y, to_z):
        return [
            pltpu.make_async_remote_copy(
                src_ref=faces.at[stage, i],
                dst_ref=halos.at[stage, i],
                send_sem=face_send.at[stage, i],
                recv_sem=face_recv.at[stage, i],
                device_id=to,
                device_id_type=MESH,
            )
            for i, to in enumerate(((to_x, gy, gz), (gx, to_y, gz), (gx, gy, to_z)))
        ]

    volume_faces = face_copies(0, before_x, before_y, (gz + s.gz - 1) % s.gz)
    flux_faces = face_copies(1, after_x, after_y, (gz + 1) % s.gz)

    def send_faces():
        def step(i, face):
            for j in range(unroll):
                y = i * unroll + j
                face = jnp.where(lane == y, pltpu.roll(volume[y], y, 1), face)
            return face

        faces[0, 0, : s.bz] = lax.fori_loop(
            0, s.by // unroll, step, jnp.zeros((s.bz, 128), jnp.float32)
        )
        faces[0, 1, : s.bz] = volume[0]
        faces[0, 2, : s.by] = volume[: s.by, 0, :]
        for copy in volume_faces:
            copy.start()

    def fluxes_inside():
        for copy in volume_faces:
            copy.wait()
        volume[s.by] = jnp.where(gy == s.gy - 1, volume[s.by - 1], halos[0, 1, : s.bz])
        last_z = (row == s.bz - 1) & (gz == s.gz - 1)
        last_x = (lane == 127) & (gx == s.gx - 1)
        scale = step_size * tv_weight

        def one(y, before, face):
            v = volume[y]
            ahead_z = jnp.where(
                row == s.bz - 1, halos[0, 2, pl.ds(y, 1), :], pltpu.roll(v, s.bz - 1, 0)
            )
            ahead_x = jnp.where(
                lane == 127, pltpu.roll(halos[0, 0, : s.bz], 127 - y, 1), pltpu.roll(v, 127, 1)
            )
            slope_y = volume[y + 1] - v
            slope_z = jnp.where(last_z, 0.0, ahead_z - v)
            slope_x = jnp.where(last_x, 0.0, ahead_x - v)
            squares = slope_y * slope_y + slope_z * slope_z + slope_x * slope_x + smoothing
            scaled = weights[y] * lax.rsqrt(squares)
            flux_y, flux_z, flux_x = scaled * slope_y, scaled * slope_z, scaled * slope_x
            gradient = before - flux_y
            gradient = gradient + jnp.where(row == 0, 0.0, pltpu.roll(flux_z, 1, 0)) - flux_z
            gradient = gradient + jnp.where(lane == 0, 0.0, pltpu.roll(flux_x, 1, 1)) - flux_x
            faces[1, 2, pl.ds(y, 1), :] = flux_z[s.bz - 1 :]
            out[y // s.classes, y % s.classes] = v - scale * gradient
            return flux_y, jnp.where(lane == y, pltpu.roll(flux_x, y + 1, 1), face)

        def step(i, carry):
            for j in range(unroll):
                carry = one(i * unroll + j, *carry)
            return carry

        zero = jnp.zeros((s.bz, 128), jnp.float32)
        flux_y, face = lax.fori_loop(0, s.by // unroll, step, (zero, zero))
        faces[1, 0, : s.bz] = face
        faces[1, 1, : s.bz] = flux_y
        for copy in flux_faces:
            copy.start()

    def take_fluxes():
        scale = step_size * tv_weight
        for copy in flux_faces:
            copy.wait()
        out[0, 0] = out[0, 0] - jnp.where(gy == 0, 0.0, scale) * halos[1, 1, : s.bz]

    def first_classes(k, _):
        @pl.when(k == 0)
        def _():
            for copy in (load_sr, load_si, load_ty):
                copy.wait()

        def wait_tx():
            @pl.when(k == 0)
            def _():
                load_tx.wait()

        transform(0, k, wait_tx)

        @pl.when(k == 0)
        def _():
            pl.semaphore_wait(barrier, s.plane - 1 + s.gz - 1)

        send_class(0, k, 1)

        @pl.when(k == 0)
        def _():
            for copy in copies[4:]:
                copy.start()
            load_volume.wait()
            send_faces()

        return 0

    def transform_class(r):
        lax.fori_loop(0, s.planes, lambda k, _: (transform(r, k), 0)[1], 0)

    lax.fori_loop(0, s.planes, first_classes, 0)
    for later in range(1, s.classes):
        transform_class(later)
        send_class(later, 0, s.planes)

    width = 2 * s.chips
    far_first = sorted(range(1, s.gz), key=lambda i: (-min(i, s.gz - i), i))

    def forward(r):
        for position, turn in enumerate(turns + [0]):
            source = (ring + s.ring - turn) % s.ring
            group = blocks.at[r, :, pl.ds(source * width, width)]
            pltpu.make_async_copy(group, group, recv1.at[r, source]).wait()

            def step(i, _):
                pltpu.make_async_remote_copy(
                    src_ref=blocks.at[r, :, pl.ds(source * width, width), (gz + i) % s.gz],
                    dst_ref=pencils.at[r, source, gz],
                    send_sem=send2,
                    recv_sem=recv2.at[r],
                    device_id=beside(i),
                    device_id_type=MESH,
                ).start()
                return 0

            for i in far_first:
                step(i, 0)
            pltpu.make_async_copy(
                blocks.at[r, :, pl.ds(source * width, width), gz],
                pencils.at[r, source, gz],
                recv2.at[r],
            ).start()

    tile_z = min(256, s.nz)

    def transform_z(r, first):
        pieces = [
            split(pencils[r, :, :, :, :, first + j, :].reshape(s.lines, 128)) for j in range(2)
        ]
        high = jnp.concatenate([p[0] for p in pieces], axis=1)
        low = jnp.concatenate([p[1] for p in pieces], axis=1)
        for t in range(s.nz // tile_z):
            at = slice(t * tile_z, (t + 1) * tile_z)
            o = dot3(tz[0, at, :], tz[1, at, :], high, low)
            for j in range(2):
                lines[r, first + j, at, :] = o[:, j * 128 : (j + 1) * 128]

        def step(i, _):
            to = (gz + i) % s.gz
            pltpu.make_async_remote_copy(
                src_ref=lines.at[r, pl.ds(first, 2), pl.ds(to * s.bz, s.bz), :],
                dst_ref=bricks.at[r, gz, pl.ds(first, 2)],
                send_sem=send3,
                recv_sem=recv3.at[r],
                device_id=beside(i),
                device_id_type=MESH,
            ).start()
            return 0

        for i in far_first:
            step(i, 0)
        pltpu.make_async_copy(
            lines.at[r, pl.ds(first, 2), pl.ds(gz * s.bz, s.bz), :],
            bricks.at[r, gz, pl.ds(first, 2)],
            recv3.at[r],
        ).start()

    def store_class(r):
        return pltpu.make_async_copy(out.at[:, r], result.at[:, r], store.at[r])

    def finish_class(r):
        pltpu.make_async_copy(bricks.at[r], bricks.at[r], recv3.at[r]).wait()

        def some_rows(i, _):
            for j in range(unroll):
                m = i * unroll + j
                y = m * s.classes + r
                x_flux = pltpu.roll(halos[1, 0, : s.bz], (128 - y) % 128, 1)
                outer = jnp.where((lane == 0) & (gx > 0), x_flux, 0.0) + jnp.where(
                    (row == 0) & (gz > 0), halos[1, 2, pl.ds(y, 1), :], 0.0
                )
                data = bricks[r, m // s.rows, m % s.rows]
                out[m, r] = out[m, r] - step_size * (data + tv_weight * outer)
            return 0

        lax.fori_loop(0, s.gz * s.rows // unroll, some_rows, 0)
        store_class(r).start()

    def gather_class(r, _):
        forward(r)

        @pl.when(r == 0)
        def _():
            load_tz.wait()

        pltpu.make_async_copy(pencils.at[r], pencils.at[r], recv2.at[r]).wait()
        for first in range(0, s.rows, 2):
            transform_z(r, first)

        @pl.when(r == 0)
        def _():
            load_weights.wait()
            fluxes_inside()

        @pl.when(r == s.classes - 1)
        def _():
            take_fluxes()
            for ready in range(s.classes - 1):
                finish_class(ready)

        return 0

    lax.fori_loop(0, s.classes, gather_class, 0)
    finish_class(s.classes - 1)
    for ready in range(s.classes):
        store_class(ready).wait()

    sent = mine.at[:, pl.ds(0, s.plane - 1)]
    pltpu.make_async_copy(sent, sent, send1).wait()
    sent = pencils.at[:, :, pl.ds(0, s.gz - 1)]
    pltpu.make_async_copy(sent, sent, send2).wait()
    sent = bricks.at[:, pl.ds(0, s.gz - 1)]
    pltpu.make_async_copy(sent, sent, send3).wait()


def deliver_kernel(source, to, held, taken, done):
    rows = source.shape[0] // DELIVERIES
    parts = [pl.ds(i * rows, rows) for i in range(DELIVERIES)]
    take = [
        pltpu.make_async_copy(source.at[part], held.at[part], taken.at[i])
        for i, part in enumerate(parts)
    ]
    give = [
        pltpu.make_async_copy(held.at[part], to.at[part], done.at[i])
        for i, part in enumerate(parts)
    ]
    for copy in take:
        copy.start()
    for first, second in zip(take, give):
        first.wait()
        second.start()
    for copy in give:
        copy.wait()


def deliver(x):
    return pl.pallas_call(
        deliver_kernel,
        out_shape=jax.ShapeDtypeStruct(x.shape, x.dtype),
        in_specs=[pl.BlockSpec(memory_space=pl.ANY)],
        out_specs=pl.BlockSpec(memory_space=pl.ANY),
        scratch_shapes=[
            pltpu.VMEM(x.shape, x.dtype),
            pltpu.SemaphoreType.DMA((DELIVERIES,)),
            pltpu.SemaphoreType.DMA((DELIVERIES,)),
        ],
    )(x)


def on_device(s, spectrum_real, spectrum_imag, volume, weights):
    tables = [jnp.asarray(t) for t in make_tables(s)]

    def rows(x):
        x = x.reshape(s.ny, s.planes, s.nx // 128, 128)
        return x.transpose(0, 2, 1, 3).reshape(s.classes, -1, 128)

    f32, bf16 = jnp.float32, jnp.bfloat16
    brick = (s.by, s.bz, s.bx)
    classed = (s.by // s.classes, s.classes, s.bz, s.bx)
    spectrum = (s.classes, s.class_y * s.planes * s.nx // 128, 128)
    face = max(s.by, s.bz)
    dma = pltpu.SemaphoreType.DMA
    updated = pl.pallas_call(
        functools.partial(kernel, s),
        out_shape=jax.ShapeDtypeStruct(classed, f32),
        in_specs=[pl.BlockSpec(memory_space=pl.ANY)] * 7,
        out_specs=pl.BlockSpec(memory_space=pl.ANY),
        scratch_shapes=[
            pltpu.VMEM(spectrum, f32),
            pltpu.VMEM(spectrum, f32),
            *(pltpu.VMEM(table.shape, bf16) for table in tables),
            pltpu.VMEM((s.by + 1, s.bz, s.bx), f32),
            pltpu.VMEM(brick, f32),
            pltpu.VMEM(classed, f32),
            pltpu.VMEM((s.classes, s.plane, s.planes, 2, s.gz, s.rows, 128), f32),
            pltpu.VMEM((s.classes, s.planes, 2 * s.plane, s.gz, s.rows, 128), f32),
            pltpu.VMEM((s.classes, s.ring, s.gz, s.planes, 2 * s.chips, s.rows, 128), f32),
            pltpu.VMEM((s.classes, s.rows, s.nz, 128), f32),
            pltpu.VMEM((s.classes, s.gz, s.rows, s.bz, 128), f32),
            pltpu.VMEM((2, 3, face, 128), f32),
            pltpu.VMEM((2, 3, face, 128), f32),
            dma,
            dma((s.classes, s.ring)),
            dma,
            dma((s.classes,)),
            dma,
            dma((s.classes,)),
            dma((7,)),
            dma((s.classes,)),
            dma((2, 3)),
            dma((2, 3)),
        ],
        compiler_params=pltpu.CompilerParams(
            collective_id=0, has_side_effects=True, vmem_limit_bytes=62 * 1024 * 1024
        ),
    )(rows(spectrum_real), rows(spectrum_imag), *tables, volume, weights)
    return deliver(updated.reshape(brick))


def build(mesh, x_chips, shape):
    sizes = Sizes([mesh.shape[a] for a in ("gx", "gy", "gz")], x_chips, *shape)
    spectrum, brick = P(None, ("gx", "gy", "gz"), None), P("gy", "gz", "gx")
    return jax.shard_map(
        functools.partial(on_device, sizes),
        mesh=mesh,
        in_specs=(spectrum, spectrum, brick, brick),
        out_specs=brick,
        check_vma=False,
    )


def solution(mesh):
    return build(mesh, X_CHIPS, (512, 512, 512))
```

```python
import functools
import math

import jax
import jax.numpy as jnp
import ml_dtypes
import numpy as np
from jax import lax
from jax.experimental import pallas as pl
from jax.experimental.pallas import tpu as pltpu
from jax.sharding import PartitionSpec as P

step_size = 0.5
tv_weight = 0.5
smoothing = 0.5
MESH = pl.DeviceIdType.MESH
X_CHIPS = 4
CLASSES = 4
DELIVERIES = 8


def halves(table):
    high = table.astype(ml_dtypes.bfloat16)
    low = (table - high.astype(np.float64)).astype(ml_dtypes.bfloat16)
    return np.stack([high, low])


def cos_sin(length, rows, columns):
    phases = (np.asarray(rows)[:, None] * np.asarray(columns)[None, :]) % length
    angles = phases * (2.0 * math.pi / length)
    factor = 1.0 / math.sqrt(length)
    return np.cos(angles) * factor, np.sin(angles) * factor


class Sizes:
    def __init__(self, mesh_sizes, x_chips, ny, nz, nx):
        self.gx, self.gy, self.gz = mesh_sizes
        self.ny, self.nz, self.nx = ny, nz, nx
        self.plane = self.gx * self.gy
        self.planes = nz // (self.plane * self.gz)
        self.chips = x_chips
        self.ring = self.plane // x_chips
        self.by, self.bz, self.bx = ny // self.gy, nz // self.gz, nx // self.gx
        self.classes = CLASSES
        self.class_y = ny // self.classes
        self.rows = self.by // (self.gz * self.classes)
        self.lines = 2 * nz


def make_tables(s):
    c, n = cos_sin(s.nx, range(s.nx), range(s.nx))
    table_x = halves(np.concatenate([c, n], axis=0))
    table_y = []
    for r in range(s.classes):
        c, n = cos_sin(s.ny, range(r, s.ny, s.classes), range(s.class_y))
        table_y.append(halves(np.concatenate([c, n], axis=1)))
    table_y = np.stack(table_y)
    r, g, k, x = np.meshgrid(
        range(s.ring), range(s.gz), range(s.planes), range(s.chips), indexing="ij"
    )
    kz = (((r * s.chips + x) * s.gz + g) * s.planes + k).reshape(-1)
    c, n = cos_sin(s.nz, range(s.nz), kz)
    table_z = halves(np.stack([c, -n], axis=-1).reshape(s.nz, s.lines))
    return table_x, table_y, table_z


def class_of(r, re, im):
    r = jnp.asarray(r, jnp.int32)
    if len(re) == 2:
        sign = (1 - 2 * r).astype(jnp.float32)
        return re[0] + sign * re[1], im[0] + sign * im[1]
    odd = r % 2
    pair = (1 - 2 * odd).astype(jnp.float32)
    sign = (1 - 2 * (r // 2)).astype(jnp.float32)
    even_sign, odd_sign = sign * (1 - odd).astype(jnp.float32), sign * odd.astype(jnp.float32)
    re_1, im_1 = re[1] + pair * re[3], im[1] + pair * im[3]
    re_0, im_0 = re[0] + pair * re[2], im[0] + pair * im[2]
    return re_0 + even_sign * re_1 - odd_sign * im_1, im_0 + even_sign * im_1 + odd_sign * re_1


def split(x):
    high = x.astype(jnp.bfloat16)
    return high, (x - high.astype(jnp.float32)).astype(jnp.bfloat16)


def dot3(a_high, a_low, b_high, b_low):
    f32 = jnp.float32
    return (
        jnp.dot(a_high, b_high, preferred_element_type=f32)
        + jnp.dot(a_high, b_low, preferred_element_type=f32)
        + jnp.dot(a_low, b_high, preferred_element_type=f32)
    )


def kernel(
    s, sr_hbm, si_hbm, tx_hbm, ty_hbm, tz_hbm, volume_hbm, weights_hbm, result,
    sr, si, tx, ty, tz, volume, weights,
    out, mine, blocks, pencils, lines, bricks, faces, halos,
    send1, recv1, send2, recv2, send3, recv3, load, store, face_send, face_recv,
):
    load_sr, load_si, load_ty, load_tx, load_volume, load_weights, load_tz = copies = [
        pltpu.make_async_copy(source, to, load.at[i])
        for i, (source, to) in enumerate(
            (
                (sr_hbm, sr),
                (si_hbm, si),
                (ty_hbm, ty),
                (tx_hbm, tx),
                (volume_hbm, volume.at[pl.ds(0, s.by)]),
                (weights_hbm, weights),
                (tz_hbm, tz),
            )
        )
    ]
    for copy in copies[:4]:
        copy.start()
    gx, gy, gz = lax.axis_index("gx"), lax.axis_index("gy"), lax.axis_index("gz")
    here = gx * s.gy + gy
    ring, chip = here // s.chips, here % s.chips
    lanes = s.nx // 128
    class_y = s.class_y

    def place(index):
        return (index // s.gy, index % s.gy, gz)

    def beside(step):
        return (gx, gy, (gz + step) % s.gz)

    barrier = pltpu.get_barrier_semaphore()

    def greet(i, _):
        pl.semaphore_signal(barrier, inc=1, device_id=place((here + i) % s.plane), device_id_type=MESH)
        return 0

    def greet_beside(i, _):
        pl.semaphore_signal(barrier, inc=1, device_id=beside(i), device_id_type=MESH)
        return 0

    for i in range(1, s.plane):
        greet(i, 0)
    for i in range(1, s.gz):
        greet_beside(i, 0)

    def transform(r, k, before_x=None):
        def quarters(ref):
            return [
                jnp.concatenate(
                    [
                        ref[q, pl.ds(k + j * s.planes, class_y, stride=lanes * s.planes), :]
                        for j in range(lanes)
                    ],
                    axis=1,
                )
                for q in range(s.classes)
            ]

        re, im = class_of(r, quarters(sr), quarters(si))
        re_high, re_low = split(re)
        im_high, im_low = split(im)
        y_high, y_low = ty[r, 0], ty[r, 1]
        real = dot3(
            y_high, y_low, jnp.concatenate([re_high, -im_high]), jnp.concatenate([re_low, -im_low])
        )
        imag = dot3(
            y_high, y_low, jnp.concatenate([im_high, re_high]), jnp.concatenate([im_low, re_low])
        )
        if before_x is not None:
            before_x()
        re_high, re_low = split(real)
        im_high, im_low = split(imag)
        high = jnp.concatenate(
            [jnp.concatenate([re_high, -im_high], 1), jnp.concatenate([im_high, re_high], 1)], 0
        )
        low = jnp.concatenate(
            [jnp.concatenate([re_low, -im_low], 1), jnp.concatenate([im_low, re_low], 1)], 0
        )
        both = dot3(high, low, tx[0], tx[1])
        for c in range(2):
            for q in range(s.gx):
                mine[r, q * s.gy : (q + 1) * s.gy, k, c] = both[
                    c * class_y : (c + 1) * class_y, q * 128 : (q + 1) * 128
                ].reshape(s.gy, s.gz, s.rows, 128)

    turns = []
    for h in range(1, s.ring // 2 + 1):
        turns += [h] if 2 * h == s.ring else [h, s.ring - h]

    far_chips = sorted(range(1, s.chips), key=lambda i: (-min(i, s.chips - i), i))

    def send_block(r, planes, turn, dx):
        to = ((ring + turn) % s.ring) * s.chips + (chip + dx) % s.chips
        pltpu.make_async_remote_copy(
            src_ref=mine.at[r, to, planes],
            dst_ref=blocks.at[r, planes, pl.ds(2 * here, 2)],
            send_sem=send1,
            recv_sem=recv1.at[r, ring],
            device_id=place(to),
            device_id_type=MESH,
        ).start()

    def send_class(r, first, planes):
        planes = pl.ds(first, planes)
        for turn in turns:
            for dx in far_chips + [0]:
                send_block(r, planes, turn, dx)
        for dx in far_chips:
            send_block(r, planes, 0, dx)
        pltpu.make_async_copy(
            mine.at[r, here, planes], blocks.at[r, planes, pl.ds(2 * here, 2)], recv1.at[r, ring]
        ).start()

    before_x, after_x = (gx + s.gx - 1) % s.gx, (gx + 1) % s.gx
    before_y, after_y = (gy + s.gy - 1) % s.gy, (gy + 1) % s.gy
    lane = lax.broadcasted_iota(jnp.int32, (s.bz, 128), 1)
    row = lax.broadcasted_iota(jnp.int32, (s.bz, 128), 0)
    unroll = 4

    def face_copies(stage, to_x, to_y, to_z):
        return [
            pltpu.make_async_remote_copy(
                src_ref=faces.at[stage, i],
                dst_ref=halos.at[stage, i],
                send_sem=face_send.at[stage, i],
                recv_sem=face_recv.at[stage, i],
                device_id=to,
                device_id_type=MESH,
            )
            for i, to in enumerate(((to_x, gy, gz), (gx, to_y, gz), (gx, gy, to_z)))
        ]

    volume_faces = face_copies(0, before_x, before_y, (gz + s.gz - 1) % s.gz)
    flux_faces = face_copies(1, after_x, after_y, (gz + 1) % s.gz)

    def send_faces():
        def step(i, face):
            for j in range(unroll):
                y = i * unroll + j
                face = jnp.where(lane == y, pltpu.roll(volume[y], y, 1), face)
            return face

        faces[0, 0, : s.bz] = lax.fori_loop(
            0, s.by // unroll, step, jnp.zeros((s.bz, 128), jnp.float32)
        )
        faces[0, 1, : s.bz] = volume[0]
        faces[0, 2, : s.by] = volume[: s.by, 0, :]
        for copy in volume_faces:
            copy.start()

    def fluxes_inside():
        for copy in volume_faces:
            copy.wait()
        volume[s.by] = jnp.where(gy == s.gy - 1, volume[s.by - 1], halos[0, 1, : s.bz])
        last_z = (row == s.bz - 1) & (gz == s.gz - 1)
        last_x = (lane == 127) & (gx == s.gx - 1)
        scale = step_size * tv_weight

        def one(y, before, face):
            v = volume[y]
            ahead_z = jnp.where(
                row == s.bz - 1, halos[0, 2, pl.ds(y, 1), :], pltpu.roll(v, s.bz - 1, 0)
            )
            ahead_x = jnp.where(
                lane == 127, pltpu.roll(halos[0, 0, : s.bz], 127 - y, 1), pltpu.roll(v, 127, 1)
            )
            slope_y = volume[y + 1] - v
            slope_z = jnp.where(last_z, 0.0, ahead_z - v)
            slope_x = jnp.where(last_x, 0.0, ahead_x - v)
            squares = slope_y * slope_y + slope_z * slope_z + slope_x * slope_x + smoothing
            scaled = weights[y] * lax.rsqrt(squares)
            flux_y, flux_z, flux_x = scaled * slope_y, scaled * slope_z, scaled * slope_x
            gradient = before - flux_y
            gradient = gradient + jnp.where(row == 0, 0.0, pltpu.roll(flux_z, 1, 0)) - flux_z
            gradient = gradient + jnp.where(lane == 0, 0.0, pltpu.roll(flux_x, 1, 1)) - flux_x
            faces[1, 2, pl.ds(y, 1), :] = flux_z[s.bz - 1 :]
            out[y // s.classes, y % s.classes] = v - scale * gradient
            return flux_y, jnp.where(lane == y, pltpu.roll(flux_x, y + 1, 1), face)

        def step(i, carry):
            for j in range(unroll):
                carry = one(i * unroll + j, *carry)
            return carry

        zero = jnp.zeros((s.bz, 128), jnp.float32)
        flux_y, face = lax.fori_loop(0, s.by // unroll, step, (zero, zero))
        faces[1, 0, : s.bz] = face
        faces[1, 1, : s.bz] = flux_y
        for copy in flux_faces:
            copy.start()

    def take_fluxes():
        scale = step_size * tv_weight
        for copy in flux_faces:
            copy.wait()
        out[0, 0] = out[0, 0] - jnp.where(gy == 0, 0.0, scale) * halos[1, 1, : s.bz]

    def first_classes(k, _):
        @pl.when(k == 0)
        def _():
            for copy in (load_sr, load_si, load_ty):
                copy.wait()

        def wait_tx():
            @pl.when(k == 0)
            def _():
                load_tx.wait()

        transform(0, k, wait_tx)

        @pl.when(k == 0)
        def _():
            pl.semaphore_wait(barrier, s.plane - 1 + s.gz - 1)

        send_class(0, k, 1)

        @pl.when(k == 0)
        def _():
            for copy in copies[4:]:
                copy.start()
            load_volume.wait()
            send_faces()

        return 0

    def transform_class(r):
        lax.fori_loop(0, s.planes, lambda k, _: (transform(r, k), 0)[1], 0)

    lax.fori_loop(0, s.planes, first_classes, 0)
    for later in range(1, s.classes):
        transform_class(later)
        send_class(later, 0, s.planes)

    width = 2 * s.chips
    far_first = sorted(range(1, s.gz), key=lambda i: (-min(i, s.gz - i), i))

    def forward(r):
        for position, turn in enumerate(turns + [0]):
            source = (ring + s.ring - turn) % s.ring
            group = blocks.at[r, :, pl.ds(source * width, width)]
            pltpu.make_async_copy(group, group, recv1.at[r, source]).wait()

            def step(i, _):
                pltpu.make_async_remote_copy(
                    src_ref=blocks.at[r, :, pl.ds(source * width, width), (gz + i) % s.gz],
                    dst_ref=pencils.at[r, source, gz],
                    send_sem=send2,
                    recv_sem=recv2.at[r],
                    device_id=beside(i),
                    device_id_type=MESH,
                ).start()
                return 0

            for i in far_first:
                step(i, 0)
            pltpu.make_async_copy(
                blocks.at[r, :, pl.ds(source * width, width), gz],
                pencils.at[r, source, gz],
                recv2.at[r],
            ).start()

    tile_z = min(256, s.nz)

    def transform_z(r, first):
        pieces = [
            split(pencils[r, :, :, :, :, first + j, :].reshape(s.lines, 128)) for j in range(2)
        ]
        high = jnp.concatenate([p[0] for p in pieces], axis=1)
        low = jnp.concatenate([p[1] for p in pieces], axis=1)
        for t in range(s.nz // tile_z):
            at = slice(t * tile_z, (t + 1) * tile_z)
            o = dot3(tz[0, at, :], tz[1, at, :], high, low)
            for j in range(2):
                lines[r, first + j, at, :] = o[:, j * 128 : (j + 1) * 128]

        def step(i, _):
            to = (gz + i) % s.gz
            pltpu.make_async_remote_copy(
                src_ref=lines.at[r, pl.ds(first, 2), pl.ds(to * s.bz, s.bz), :],
                dst_ref=bricks.at[r, gz, pl.ds(first, 2)],
                send_sem=send3,
                recv_sem=recv3.at[r],
                device_id=beside(i),
                device_id_type=MESH,
            ).start()
            return 0

        for i in far_first:
            step(i, 0)
        pltpu.make_async_copy(
            lines.at[r, pl.ds(first, 2), pl.ds(gz * s.bz, s.bz), :],
            bricks.at[r, gz, pl.ds(first, 2)],
            recv3.at[r],
        ).start()

    def store_class(r):
        return pltpu.make_async_copy(out.at[:, r], result.at[:, r], store.at[r])

    def finish_class(r):
        pltpu.make_async_copy(bricks.at[r], bricks.at[r], recv3.at[r]).wait()

        def some_rows(i, _):
            for j in range(unroll):
                m = i * unroll + j
                y = m * s.classes + r
                x_flux = pltpu.roll(halos[1, 0, : s.bz], (128 - y) % 128, 1)
                outer = jnp.where((lane == 0) & (gx > 0), x_flux, 0.0) + jnp.where(
                    (row == 0) & (gz > 0), halos[1, 2, pl.ds(y, 1), :], 0.0
                )
                data = bricks[r, m // s.rows, m % s.rows]
                out[m, r] = out[m, r] - step_size * (data + tv_weight * outer)
            return 0

        lax.fori_loop(0, s.gz * s.rows // unroll, some_rows, 0)
        store_class(r).start()

    def gather_class(r, _):
        forward(r)

        @pl.when(r == 0)
        def _():
            load_tz.wait()

        pltpu.make_async_copy(pencils.at[r], pencils.at[r], recv2.at[r]).wait()
        for first in range(0, s.rows, 2):
            transform_z(r, first)

        @pl.when(r == 0)
        def _():
            load_weights.wait()
            fluxes_inside()

        @pl.when(r == s.classes - 1)
        def _():
            take_fluxes()
            for ready in range(s.classes - 1):
                finish_class(ready)

        return 0

    lax.fori_loop(0, s.classes, gather_class, 0)
    finish_class(s.classes - 1)
    for ready in range(s.classes):
        store_class(ready).wait()

    sent = mine.at[:, pl.ds(0, s.plane - 1)]
    pltpu.make_async_copy(sent, sent, send1).wait()
    sent = pencils.at[:, :, pl.ds(0, s.gz - 1)]
    pltpu.make_async_copy(sent, sent, send2).wait()
    sent = bricks.at[:, pl.ds(0, s.gz - 1)]
    pltpu.make_async_copy(sent, sent, send3).wait()


def deliver_kernel(source, to, held, taken, done):
    rows = source.shape[0] // DELIVERIES
    parts = [pl.ds(i * rows, rows) for i in range(DELIVERIES)]
    take = [
        pltpu.make_async_copy(source.at[part], held.at[part], taken.at[i])
        for i, part in enumerate(parts)
    ]
    give = [
        pltpu.make_async_copy(held.at[part], to.at[part], done.at[i])
        for i, part in enumerate(parts)
    ]
    for copy in take:
        copy.start()
    for first, second in zip(take, give):
        first.wait()
        second.start()
    for copy in give:
        copy.wait()


def deliver(x):
    return pl.pallas_call(
        deliver_kernel,
        out_shape=jax.ShapeDtypeStruct(x.shape, x.dtype),
        in_specs=[pl.BlockSpec(memory_space=pl.ANY)],
        out_specs=pl.BlockSpec(memory_space=pl.ANY),
        scratch_shapes=[
            pltpu.VMEM(x.shape, x.dtype),
            pltpu.SemaphoreType.DMA((DELIVERIES,)),
            pltpu.SemaphoreType.DMA((DELIVERIES,)),
        ],
    )(x)


def on_device(s, spectrum_real, spectrum_imag, volume, weights):
    tables = [jnp.asarray(t) for t in make_tables(s)]

    def rows(x):
        x = x.reshape(s.ny, s.planes, s.nx // 128, 128)
        return x.transpose(0, 2, 1, 3).reshape(s.classes, -1, 128)

    f32, bf16 = jnp.float32, jnp.bfloat16
    brick = (s.by, s.bz, s.bx)
    classed = (s.by // s.classes, s.classes, s.bz, s.bx)
    spectrum = (s.classes, s.class_y * s.planes * s.nx // 128, 128)
    face = max(s.by, s.bz)
    dma = pltpu.SemaphoreType.DMA
    updated = pl.pallas_call(
        functools.partial(kernel, s),
        out_shape=jax.ShapeDtypeStruct(classed, f32),
        in_specs=[pl.BlockSpec(memory_space=pl.ANY)] * 7,
        out_specs=pl.BlockSpec(memory_space=pl.ANY),
        scratch_shapes=[
            pltpu.VMEM(spectrum, f32),
            pltpu.VMEM(spectrum, f32),
            *(pltpu.VMEM(table.shape, bf16) for table in tables),
            pltpu.VMEM((s.by + 1, s.bz, s.bx), f32),
            pltpu.VMEM(brick, f32),
            pltpu.VMEM(classed, f32),
            pltpu.VMEM((s.classes, s.plane, s.planes, 2, s.gz, s.rows, 128), f32),
            pltpu.VMEM((s.classes, s.planes, 2 * s.plane, s.gz, s.rows, 128), f32),
            pltpu.VMEM((s.classes, s.ring, s.gz, s.planes, 2 * s.chips, s.rows, 128), f32),
            pltpu.VMEM((s.classes, s.rows, s.nz, 128), f32),
            pltpu.VMEM((s.classes, s.gz, s.rows, s.bz, 128), f32),
            pltpu.VMEM((2, 3, face, 128), f32),
            pltpu.VMEM((2, 3, face, 128), f32),
            dma,
            dma((s.classes, s.ring)),
            dma,
            dma((s.classes,)),
            dma,
            dma((s.classes,)),
            dma((7,)),
            dma((s.classes,)),
            dma((2, 3)),
            dma((2, 3)),
        ],
        compiler_params=pltpu.CompilerParams(
            collective_id=0, has_side_effects=True, vmem_limit_bytes=62 * 1024 * 1024
        ),
    )(rows(spectrum_real), rows(spectrum_imag), *tables, volume, weights)
    return deliver(updated.reshape(brick))


def build(mesh, x_chips, shape):
    sizes = Sizes([mesh.shape[a] for a in ("gx", "gy", "gz")], x_chips, *shape)
    spectrum, brick = P(None, ("gx", "gy", "gz"), None), P("gy", "gz", "gx")
    return jax.shard_map(
        functools.partial(on_device, sizes),
        mesh=mesh,
        in_specs=(spectrum, spectrum, brick, brick),
        out_specs=brick,
        check_vma=False,
    )


def solution(mesh):
    return build(mesh, X_CHIPS, (512, 512, 512))
```
